256 devices in a mesh: section: 8 (over y, z_hi), tp: 32 (over x, z_lo, core).
Axes of the slice: x: 4, y: 4, z: 8 (z_hi: 2, z_lo: 4; z = z_hi * 4 + z_lo), core: 2. Of those that a mesh axis runs over, the one named last changes fastest.
Arguments:
- scan_input: bfloat16 [2048, 16384], P('section', 'tp'), may hold values from -6 to 6
- input_map: bfloat16 [2048, 1024], P('section'), may hold values from -0.375 to 0.375
- output_map: bfloat16 [2048, 1024], P('section'), may hold values from -0.375 to 0.375
- log_decay: float32 [2048, 256], P('section', 'tp'), may hold values from -0.6 to 0
- skip_gain: float32 [256], P('tp'), may hold values from 0.5 to 2
- query_rows: bfloat16 [2048, 8192], P('section', 'tp'), may hold values from -10 to 10
- key_rows: bfloat16 [2048, 1024], P('section'), may hold values from -10 to 10
- value_rows: bfloat16 [2048, 1024], P('section'), may hold values from -15 to 15
- out_weight: bfloat16 [8192, 8192], P(None, 'tp'), may hold values from -0.5 to 0.5
Outputs:
- ssm_out: bfloat16 [2048, 16384], P('section', 'tp')
- attn_out: bfloat16 [8192, 2048], P('tp', 'section')
The draws below stay inside these ranges and needn't reach their ends.
All inputs are finite; a program needn't handle non-finite values.
Results may differ from the reference program's by a relative error of at most 0.0075.
Values may be sent and summed in bfloat16 or wider, within the bound.
No kernel may reach another device: no remote copies, remote signals or barrier semaphores. Data moves between devices by JAX's collectives and lax.ppermute only.
A program may use at most 64 MiB of HBM per device.

```python
import math
import jax
import jax.numpy as jnp
from jax import lax

D_MODEL = 8192
SCAN_HEADS = 256
SSM_HEAD_DIM = 64
N_STATE = 128
GROUPS = 8
Q_HEADS = 64
KV_HEADS = 8
HEAD_DIM = 128
BLOCK = 128
PROMPT_TOKENS = 2048


def draw_query_rows(key, part):
    own_key = jax.random.fold_in(key, 21)
    base = jnp.clip(1.5 * jax.random.normal(own_key, (PROMPT_TOKENS, Q_HEADS * HEAD_DIM), jnp.float32), -9.0, 9.0)
    return base.astype(jnp.bfloat16)


def draw_key_rows(key, part):
    own_key = jax.random.fold_in(key, 22)
    base = jnp.clip(jax.random.normal(own_key, (PROMPT_TOKENS, KV_HEADS * HEAD_DIM), jnp.float32), -6.0, 6.0)
    return base.astype(jnp.bfloat16)


def draw_log_decay(key, part):
    own_key = jax.random.fold_in(key, 31)
    divided_keys = jax.random.split(own_key, 6)
    order = jax.random.permutation(divided_keys[0], SCAN_HEADS)
    fast = order < SCAN_HEADS // 2
    fast_rate = jnp.exp(jax.random.uniform(divided_keys[1], (SCAN_HEADS,), jnp.float32, math.log(1.0 / 50.0), math.log(1.0 / 30.0)))
    slow_rate = jnp.exp(jax.random.uniform(divided_keys[2], (SCAN_HEADS,), jnp.float32, math.log(0.2), math.log(0.8))) / PROMPT_TOKENS
    decay_rate = jnp.where(fast, fast_rate, slow_rate)
    coarse_values = jnp.exp(jax.random.uniform(divided_keys[3], (PROMPT_TOKENS, SCAN_HEADS), jnp.float32, -0.7, 0.7))
    block_position = jax.random.randint(divided_keys[4], (2,), 1, PROMPT_TOKENS)
    blocked_scores = jnp.any(jnp.arange(PROMPT_TOKENS)[:, None] == block_position[None, :], axis=1).astype(jnp.float32)
    block_span = jax.random.uniform(divided_keys[5], (PROMPT_TOKENS, SCAN_HEADS), jnp.float32, 0.22, 0.5) * blocked_scores[:, None]
    return -(decay_rate[None, :] * coarse_values + block_span)


def raised(entries, stream_key, source, target, parts, factor):
    owner, partner = [(jnp.arange(entries.shape[dim]) // (entries.shape[dim] // parts)).reshape([-1 if axis == dim else 1 for axis in range(entries.ndim)]) for dim in (source, target)]
    chosen = jax.random.permutation(stream_key, parts)[partner]
    strong = (owner == chosen) | (owner == (partner + parts // 2) % parts)
    return jnp.where(strong, factor * entries, entries)


def level_of(rng, shape, pieces, smallest, largest):
    def one(position, blocks):
        steps = jax.random.uniform(jax.random.fold_in(jax.random.fold_in(rng, 6), position), (blocks,), jnp.float32, smallest / len(pieces), largest / len(pieces))
        return jnp.repeat(jnp.exp(steps), shape[position] // blocks).reshape((-1,) + (1,) * (len(shape) - position - 1))

    level = one(*pieces[0])
    for cut in pieces[1:]:
        level = level * one(*cut)
    return level


def bell_draw(key, extent, spread, bound, cuts=(), held_as=jnp.bfloat16):
    entries = spread * jax.random.normal(key, extent, jnp.float32)
    if cuts:
        entries = entries * level_of(key, extent, cuts, -0.22, 0.18)
    return jnp.clip(entries, -bound, bound).astype(held_as)


def gaussian_with(rng, shape, deviation, limit, cuts, heavy, kind=jnp.bfloat16):
    values = deviation * jax.random.normal(rng, shape, jnp.float32)
    if cuts:
        values = values * level_of(rng, shape, cuts, -0.22, 0.18)
    return jnp.clip(raised(values, jax.random.fold_in(rng, 3), *heavy), -limit, limit).astype(kind)


def setup_inputs(seed: int = 0) -> dict:
    arg_keys = jax.random.split(jax.random.key(seed), 10)
    return {
        "scan_input": bell_draw(arg_keys[0], (PROMPT_TOKENS, SCAN_HEADS * SSM_HEAD_DIM), 1.0, 6.0, ((0, 8), (1, 32))),
        "input_map": bell_draw(arg_keys[1], (PROMPT_TOKENS, GROUPS * N_STATE), (2 * N_STATE) ** -0.5, 0.375, ((0, 8),)),
        "output_map": bell_draw(arg_keys[2], (PROMPT_TOKENS, GROUPS * N_STATE), (2 * N_STATE) ** -0.5, 0.375, ((0, 8),)),
        "log_decay": draw_log_decay(jax.random.fold_in(arg_keys[9], 71), 0),
        "skip_gain": jnp.clip(jnp.exp(math.log(2.0) - 1.3862944 * jax.random.uniform(arg_keys[4], (SCAN_HEADS,), jnp.float32) ** level_of(arg_keys[4], (SCAN_HEADS,), ((0, 32),), -0.2, 0.2)), 0.5, 2.0),
        "query_rows": draw_query_rows(jax.random.fold_in(arg_keys[9], 71), 0),
        "key_rows": draw_key_rows(jax.random.fold_in(arg_keys[9], 71), 0),
        "value_rows": bell_draw(arg_keys[7], (PROMPT_TOKENS, KV_HEADS * HEAD_DIM), 2.5, 15.0, ((0, 8),)),
        "out_weight": gaussian_with(arg_keys[8], (D_MODEL, Q_HEADS * HEAD_DIM), (Q_HEADS * HEAD_DIM // 16) ** -0.5, 0.5, ((1, 32),), (1, 0, 32, 2.75)),
    }


highest = lax.Precision.HIGHEST

def mixer_scan(scan_input, input_map, output_map, log_decay, skip_gain):
    blocks = PROMPT_TOKENS // BLOCK
    per_group = SCAN_HEADS // GROUPS
    inputs_all = scan_input.astype(jnp.float32).reshape(blocks, BLOCK, SCAN_HEADS, SSM_HEAD_DIM)
    in_maps = input_map.astype(jnp.float32).reshape(blocks, BLOCK, GROUPS, N_STATE)
    out_maps = output_map.astype(jnp.float32).reshape(blocks, BLOCK, GROUPS, N_STATE)
    decays = log_decay.reshape(blocks, BLOCK, SCAN_HEADS)
    causal = jnp.arange(BLOCK)[:, None] >= jnp.arange(BLOCK)[None, :]

    def advance(hidden, block_item):
        inputs, in_map, out_map, decay = block_item
        running = jnp.cumsum(decay, axis=0)
        affinity = jnp.einsum('qgn,sgn->gqs', out_map, in_map, precision=highest)
        affinity = jnp.repeat(affinity, per_group, axis=0)
        decay_gaps = running.T[:, :, None] - running.T[:, None, :]
        mixing = affinity * jnp.exp(jnp.where(causal[None], decay_gaps, -jnp.inf))
        inside = jnp.einsum('hqs,shp->qhp', mixing, inputs, precision=highest)
        out_heads = jnp.repeat(out_map, per_group, axis=1)
        in_heads = jnp.repeat(in_map, per_group, axis=1)
        carried = jnp.exp(running)[:, :, None] * jnp.einsum('qhn,hpn->qhp', out_heads, hidden, precision=highest)
        result = inside + carried + skip_gain[None, :, None] * inputs
        tail_decay = jnp.exp(running[-1][None, :] - running)
        hidden = jnp.exp(running[-1])[:, None, None] * hidden + jnp.einsum('qhp,qhn->hpn', inputs * tail_decay[:, :, None], in_heads, precision=highest)
        return (hidden, result)
    start_state = jnp.zeros((SCAN_HEADS, SSM_HEAD_DIM, N_STATE), jnp.float32)
    closing, outputs = lax.scan(advance, start_state, (inputs_all, in_maps, out_maps, decays))
    return outputs.reshape(PROMPT_TOKENS, SCAN_HEADS * SSM_HEAD_DIM).astype(jnp.bfloat16)

def attend(query_rows, key_rows, value_rows):
    per_group = Q_HEADS // KV_HEADS
    scale = 1.0 / math.sqrt(HEAD_DIM)
    causal = jnp.arange(PROMPT_TOKENS)[:, None] >= jnp.arange(PROMPT_TOKENS)[None, :]

    def one_head(head_index):
        kv_index = head_index // per_group
        query = lax.dynamic_slice_in_dim(query_rows, head_index * HEAD_DIM, HEAD_DIM, 1)
        key_part = lax.dynamic_slice_in_dim(key_rows, kv_index * HEAD_DIM, HEAD_DIM, 1)
        value_part = lax.dynamic_slice_in_dim(value_rows, kv_index * HEAD_DIM, HEAD_DIM, 1)
        scores = jnp.dot(query, key_part.T, preferred_element_type=jnp.float32) * scale
        scores = jnp.where(causal, scores, -jnp.inf)
        row_max = lax.optimization_barrier(jnp.max(scores, axis=1, keepdims=True))
        weights = jnp.exp(scores - row_max)
        row_total = lax.optimization_barrier(jnp.sum(weights, axis=1, keepdims=True))
        mixed = jnp.dot(weights.astype(jnp.bfloat16), value_part, preferred_element_type=jnp.float32) / row_total
        return mixed.astype(jnp.bfloat16)
    heads_out = lax.map(one_head, jnp.arange(Q_HEADS, dtype=jnp.int32))
    return heads_out.transpose(1, 0, 2).reshape(PROMPT_TOKENS, Q_HEADS * HEAD_DIM)

def reference(scan_input, input_map, output_map, log_decay, skip_gain, query_rows, key_rows, value_rows, out_weight):
    ssm_out = mixer_scan(scan_input, input_map, output_map, log_decay, skip_gain)
    attended = attend(query_rows, key_rows, value_rows)
    attn_out = jnp.dot(out_weight, attended.T, preferred_element_type=jnp.float32).astype(jnp.bfloat16)
    return (ssm_out, attn_out)
```

```python
import math

import jax
import jax.numpy as jnp
from jax import lax
from jax.experimental import pallas as pl
from jax.experimental.pallas import tpu as pltpu
from jax.sharding import PartitionSpec as P

SCAN_HEADS = 256
SSM_HEAD_DIM = 64
N_STATE = 128
GROUPS = 8
Q_HEADS = 64
KV_HEADS = 8
HEAD_DIM = 128

SECTIONS = 8
TP = 32
ROWS = 256
CHIPS = 16
masked_score = -1e30
bf16 = jnp.bfloat16
f32 = jnp.float32
VMEM_LIMIT = 48 * 1024 * 1024


def swap_core(block):
    return lax.ppermute(block, "tp", [(t, t ^ 1) for t in range(TP)])


def swap_zh(block):
    return lax.ppermute(block, "section", [(s, s ^ 1) for s in range(SECTIONS)])


def shift_y(block, distance):
    route = [(s, (s + 2 * distance) % SECTIONS) for s in range(SECTIONS)]
    return lax.ppermute(block, "section", route)


def swap_zh_near(block):
    route = [
        (s * TP + t, (s ^ 1) * TP + (t ^ 4)) for s in range(SECTIONS) for t in range(TP)
    ]
    return lax.ppermute(block, ("section", "tp"), route)


def swap_chip(block, offset):
    return lax.ppermute(block, "tp", [(t, t ^ (2 * offset)) for t in range(TP)])


def params():
    return pltpu.CompilerParams(vmem_limit_bytes=VMEM_LIMIT)


def whole(shape):
    return pl.BlockSpec(shape, lambda i, s: (0,) * len(shape))


def call(body, scalars, in_specs, out_shapes, args, scratch=(), flops=0, moved=0):
    return pl.pallas_call(
        body,
        grid_spec=pltpu.PrefetchScalarGridSpec(
            num_scalar_prefetch=1,
            grid=(1,),
            in_specs=in_specs,
            out_specs=[whole(o.shape) for o in out_shapes],
            scratch_shapes=list(scratch),
        ),
        out_shape=out_shapes,
        compiler_params=params(),
        cost_estimate=pl.CostEstimate(flops=flops, bytes_accessed=moved, transcendentals=0),
    )(scalars, *args)


def pick_body(s, k_own, v_own, k_far, v_far, own, far):
    @pl.when(s[2] == 0)
    def _():
        own[...] = k_own[...]
        far[...] = k_far[...]

    @pl.when(s[2] != 0)
    def _():
        own[...] = v_own[...]
        far[...] = v_far[...]


def attend_body(s, q, m0, m1, m2, m3, o0, o1, o2, o3, out, scores):
    y, zh, core = s[0], s[1], s[2]
    length = q.shape[0]
    half = m0.shape[0] // 2
    me = y * 2 + zh

    def run(keys, values):
        stacked = jnp.concatenate([q[:, :HEAD_DIM], q[:, HEAD_DIM:]], axis=0)
        top = None
        for b, key in enumerate(keys):
            for part in range(2):
                got = lax.dot_general(
                    stacked,
                    key[part * half : (part + 1) * half, :],
                    (((1,), (1,)), ((), ())),
                    preferred_element_type=f32,
                ) * (1.0 / math.sqrt(HEAD_DIM))
                if b == 0 and part == 0:
                    row = lax.broadcasted_iota(jnp.int32, got.shape, 0) & (length - 1)
                    col = lax.broadcasted_iota(jnp.int32, got.shape, 1)
                    got = jnp.where(col <= row, got, masked_score)
                else:
                    owner = ((y + 4 - b) & 3) * 2 + (zh if part == 0 else 1 - zh)
                    got = jnp.where(owner < me, got, masked_score)
                at = (2 * b + part) * half
                scores[:, at : at + half] = got
                peak = jnp.max(got, axis=1, keepdims=True)
                top = peak if top is None else jnp.maximum(top, peak)
        total = jnp.zeros_like(top)
        mixed = jnp.zeros(stacked.shape, f32)
        for b, value in enumerate(values):
            weights = jnp.exp(scores[:, 2 * half * b : 2 * half * (b + 1)] - top)
            total = total + jnp.sum(weights, axis=1, keepdims=True)
            mixed = mixed + jnp.dot(weights.astype(bf16), value[...], preferred_element_type=f32)
        done = (mixed / total).astype(bf16)
        out[:, :HEAD_DIM] = done[:length]
        out[:, HEAD_DIM:] = done[length:]

    @pl.when(core == 0)
    def _():
        run((m0, m1, m2, m3), (o0, o1, o2, o3))

    @pl.when(core != 0)
    def _():
        run((o0, o1, o2, o3), (m0, m1, m2, m3))


def project_body(count):
    def body(s, *refs):
        own = refs[:count]
        got = refs[count : 2 * count]
        here, there = refs[2 * count : 2 * count + 2]
        outs = refs[2 * count + 2 :]
        contract = (((1,), (1,)), ((), ()))
        for w, v, o in zip(own, got, outs):
            o[...] = (
                lax.dot_general(w[...], here[...], contract, preferred_element_type=f32)
                + lax.dot_general(v[...], there[...], contract, preferred_element_type=f32)
            ).astype(bf16)

    return body


def running_sums(decay):
    length = decay.shape[0]
    row = lax.broadcasted_iota(jnp.int32, (length, length), 0)
    col = lax.broadcasted_iota(jnp.int32, (length, length), 1)
    lower = (col <= row).astype(f32)
    down = jnp.dot(lower, decay, precision=lax.Precision.HIGHEST, preferred_element_type=f32)
    across = lax.dot_general(
        decay,
        lower,
        (((0,), (1,)), ((), ())),
        precision=lax.Precision.HIGHEST,
        preferred_element_type=f32,
    )
    return down, across


def widen(per_head, width):
    heads = per_head.shape[1]
    row = lax.broadcasted_iota(jnp.int32, (heads, heads * width), 0)
    col = lax.broadcasted_iota(jnp.int32, (heads, heads * width), 1)
    spread = ((col // width) == row).astype(f32)
    return jnp.dot(per_head, spread, precision=lax.Precision.HIGHEST, preferred_element_type=f32)


def closing_body(s, x, in_rows, decay, out):
    heads = decay.shape[1]
    inner = heads * SSM_HEAD_DIM
    length = x.shape[0]
    down, across = running_sums(decay[...])
    tail = widen(jnp.exp(down[length - 1 :, :] - down), SSM_HEAD_DIM)
    scaled = (x[...].astype(f32) * tail).astype(bf16)
    out[:inner, :] = lax.dot_general(
        scaled, in_rows[...], (((0,), (0,)), ((), ())), preferred_element_type=f32
    ).astype(bf16)
    fade = jnp.exp(across[:, length - 1 :])
    fade = jnp.broadcast_to(fade, (heads, N_STATE))
    high = fade.astype(bf16)
    out[inner : inner + 2 * heads, :] = jnp.concatenate(
        [high.astype(f32), fade - high.astype(f32)], axis=0
    ).astype(bf16)


def fades(state, inner, heads):
    both = state[inner : inner + 2 * heads, :].astype(f32)
    return both[:heads] + both[heads:]


def head_rows(h):
    return slice(h * SSM_HEAD_DIM, (h + 1) * SSM_HEAD_DIM)


def pair_body(heads):
    inner = heads * SSM_HEAD_DIM

    def body(s, mine, partner, out):
        def run(first, second):
            fade0 = fades(first, inner, heads)
            fade1 = fades(second, inner, heads)
            for h in range(heads):
                rows = head_rows(h)
                out[rows, :] = (
                    fade1[h : h + 1] * first[rows, :].astype(f32) + second[rows, :].astype(f32)
                ).astype(bf16)
            fade = fade0 * fade1
            high = fade.astype(bf16)
            out[inner : inner + 2 * heads, :] = jnp.concatenate(
                [high.astype(f32), fade - high.astype(f32)], axis=0
            ).astype(bf16)

        @pl.when(s[1] == 0)
        def _():
            run(mine, partner)

        @pl.when(s[1] != 0)
        def _():
            run(partner, mine)

    return body


def scan_body(s, x, in_rows, out_rows, decay, gain, partner, t1, t2, t3, out, entering):
    y, zh = s[0], s[1]
    heads = decay.shape[1]
    inner = heads * SSM_HEAD_DIM
    length = x.shape[0]
    down, across = running_sums(decay[...])
    fade1 = fades(t1, inner, heads)
    fade2 = fades(t2, inner, heads)
    fade0 = fades(partner, inner, heads)
    for h in range(heads):
        rows = head_rows(h)
        third = jnp.where(y >= 3, t3[rows, :].astype(f32), 0.0)
        second = jnp.where(y >= 2, t2[rows, :].astype(f32), 0.0)
        first = jnp.where(y >= 1, t1[rows, :].astype(f32), 0.0)
        state = first + fade1[h : h + 1] * (second + fade2[h : h + 1] * third)
        later = fade0[h : h + 1] * state + partner[rows, :].astype(f32)
        entering[rows, :] = jnp.where(zh == 0, state, later).astype(bf16)
    contract = (((1,), (1,)), ((), ()))
    wide = x[...].astype(f32)
    carried = widen(jnp.exp(down), SSM_HEAD_DIM) * lax.dot_general(
        out_rows[...], entering[...], contract, preferred_element_type=f32
    )
    rest = carried + widen(gain[...], SSM_HEAD_DIM) * wide
    affinity = lax.dot_general(
        out_rows[...], in_rows[...], contract, preferred_element_type=f32
    )
    row = lax.broadcasted_iota(jnp.int32, (length, length), 0)
    col = lax.broadcasted_iota(jnp.int32, (length, length), 1)
    causal = col <= row
    for h in range(heads):
        lanes = slice(h * SSM_HEAD_DIM, (h + 1) * SSM_HEAD_DIM)
        gaps = down[:, h : h + 1] - across[h : h + 1, :]
        mixing = affinity * jnp.exp(jnp.where(causal, gaps, masked_score))
        inside = jnp.dot(mixing.astype(bf16), x[:, lanes], preferred_element_type=f32)
        out[:, lanes] = (inside + rest[:, lanes]).astype(bf16)


def sum_body(count):
    def body(s, *refs):
        total = refs[0][...].astype(f32)
        for ref in refs[1:count]:
            total = total + ref[...].astype(f32)
        refs[count][...] = total.astype(bf16)

    return body


def on_device(
    scan_input,
    input_map,
    output_map,
    log_decay,
    skip_gain,
    query_rows,
    key_rows,
    value_rows,
    out_weight,
):
    section = lax.axis_index("section")
    tp = lax.axis_index("tp")
    y, zh = section // 2, section % 2
    core, chip = tp % 2, tp // 2
    group = tp // (TP // GROUPS)
    shape = jax.ShapeDtypeStruct
    scalars = jnp.stack(
        [y, zh, core, group, group ^ 1] + [chip ^ r for r in range(CHIPS)]
    ).astype(jnp.int32)

    length = query_rows.shape[0]
    head_block = (length, HEAD_DIM)
    own_spec = pl.BlockSpec(head_block, lambda i, s: (0, s[3]))
    far_spec = pl.BlockSpec(head_block, lambda i, s: (0, s[4]))
    block = shape(head_block, bf16)
    own, far = call(
        pick_body,
        scalars,
        [own_spec, own_spec, far_spec, far_spec],
        [block, block],
        (key_rows, value_rows, key_rows, value_rows),
        moved=6 * length * HEAD_DIM * 2,
    )
    pair = jnp.concatenate([own, swap_zh_near(far)], axis=0)

    weights = out_weight.reshape(CHIPS, 2, ROWS, out_weight.shape[1])
    sent = lax.dynamic_index_in_dim(weights, 1 - core, 1, keepdims=False)
    got_weight = swap_core(sent.reshape(CHIPS * ROWS, out_weight.shape[1]))

    heads = log_decay.shape[1]
    inner = heads * SSM_HEAD_DIM
    state_shape = shape((inner + 2 * heads, N_STATE), bf16)
    x_spec = whole(scan_input.shape)
    decay_spec = whole(log_decay.shape)
    (closing,) = call(
        closing_body,
        scalars,
        [x_spec, own_spec, decay_spec],
        [state_shape],
        (scan_input, input_map, log_decay),
        flops=2 * length * inner * N_STATE,
        moved=600000,
    )

    pairs = [pair] + [shift_y(pair, d) for d in (1, 2, 3)]
    others = [swap_core(p) for p in pairs]
    (attended,) = call(
        attend_body,
        scalars,
        [whole(query_rows.shape)] + [whole(pair.shape)] * 8,
        [shape(query_rows.shape, bf16)],
        (query_rows, *pairs, *others),
        scratch=[pltpu.VMEM((2 * length, 4 * pair.shape[0]), f32)],
        flops=4 * 2 * length * 4 * pair.shape[0] * HEAD_DIM,
        moved=2000000,
    )
    attended_there = swap_core(attended)

    partner = swap_zh(closing)
    (joined,) = call(
        pair_body(heads),
        scalars,
        [whole(closing.shape)] * 2,
        [state_shape],
        (closing, partner),
        moved=400000,
    )
    earlier = [shift_y(joined, d) for d in (1, 2, 3)]

    weight_block = (ROWS, out_weight.shape[1])
    parts = []
    for start in range(0, CHIPS, 4):
        offsets = list(range(start, start + 4))
        own_specs = [
            pl.BlockSpec(weight_block, lambda i, s, r=r: (s[5 + r] * 2 + s[2], 0)) for r in offsets
        ]
        got_specs = [pl.BlockSpec(weight_block, lambda i, s, r=r: (s[5 + r], 0)) for r in offsets]
        parts += call(
            project_body(4),
            scalars,
            own_specs + got_specs + [whole(attended.shape)] * 2,
            [shape((ROWS, length), bf16)] * 4,
            [out_weight] * 4 + [got_weight] * 4 + [attended, attended_there],
            flops=4 * 2 * ROWS * 512 * length,
            moved=2000000,
        )
    arrived = [parts[0]] + [swap_chip(parts[r], r) for r in range(1, CHIPS)]
    (attn_out,) = call(
        sum_body(CHIPS),
        scalars,
        [whole((ROWS, length))] * CHIPS,
        [shape((ROWS, length), bf16)],
        arrived,
        moved=17 * ROWS * length * 2,
    )

    (ssm_out,) = call(
        scan_body,
        scalars,
        [x_spec, own_spec, own_spec, decay_spec, whole((1, heads))]
        + [whole(closing.shape)] * 4,
        [shape(scan_input.shape, bf16)],
        (
            scan_input,
            input_map,
            output_map,
            log_decay,
            skip_gain.reshape(1, heads),
            partner,
            *earlier,
        ),
        scratch=[pltpu.VMEM((inner, N_STATE), bf16)],
        flops=2 * heads * length * length * SSM_HEAD_DIM,
        moved=1500000,
    )
    return (ssm_out, attn_out)


def solution(mesh):
    placed = (
        P("section", "tp"),
        P("section", None),
        P("section", None),
        P("section", "tp"),
        P("tp"),
        P("section", "tp"),
        P("section", None),
        P("section", None),
        P(None, "tp"),
    )
    return jax.shard_map(
        on_device,
        mesh=mesh,
        in_specs=placed,
        out_specs=(P("section", "tp"), P("tp", "section")),
        check_vma=False,
    )
```

```python
import math

import jax
import jax.numpy as jnp
from jax import lax
from jax.experimental import pallas as pl
from jax.experimental.pallas import tpu as pltpu
from jax.sharding import PartitionSpec as P

SCAN_HEADS = 256
SSM_HEAD_DIM = 64
N_STATE = 128
GROUPS = 8
Q_HEADS = 64
KV_HEADS = 8
HEAD_DIM = 128

SECTIONS = 8
TP = 32
ROWS = 256
CHIPS = 16
masked_score = -1e30
bf16 = jnp.bfloat16
f32 = jnp.float32
VMEM_LIMIT = 24 * 1024 * 1024


def swap_core(block):
    return lax.ppermute(block, "tp", [(t, t ^ 1) for t in range(TP)])


def swap_zh(block):
    return lax.ppermute(block, "section", [(s, s ^ 1) for s in range(SECTIONS)])


def shift_y(block, distance):
    route = [(s, (s + 2 * distance) % SECTIONS) for s in range(SECTIONS)]
    return lax.ppermute(block, "section", route)


def swap_zh_near(block):
    route = [
        (s * TP + t, (s ^ 1) * TP + (t ^ 4)) for s in range(SECTIONS) for t in range(TP)
    ]
    return lax.ppermute(block, ("section", "tp"), route)


def swap_x(block, offset):
    return lax.ppermute(block, "tp", [(t, t ^ (8 * offset)) for t in range(TP)])


def swap_zl(block, offset):
    return lax.ppermute(block, "tp", [(t, t ^ (2 * offset)) for t in range(TP)])


def params():
    return pltpu.CompilerParams(vmem_limit_bytes=VMEM_LIMIT)


def whole(shape):
    return pl.BlockSpec(shape, lambda i, s: (0,) * len(shape))


def call(body, scalars, in_specs, out_shapes, args, scratch=(), flops=0, moved=0, out_specs=None):
    return pl.pallas_call(
        body,
        grid_spec=pltpu.PrefetchScalarGridSpec(
            num_scalar_prefetch=1,
            grid=(1,),
            in_specs=in_specs,
            out_specs=out_specs or [whole(o.shape) for o in out_shapes],
            scratch_shapes=list(scratch),
        ),
        out_shape=out_shapes,
        compiler_params=params(),
        cost_estimate=pl.CostEstimate(flops=flops, bytes_accessed=moved, transcendentals=0),
    )(scalars, *args)


def pick_body(s, k_own, v_own, k_far, v_far, own, far):
    @pl.when(s[2] == 0)
    def _():
        own[...] = k_own[...]
        far[...] = k_far[...]

    @pl.when(s[2] != 0)
    def _():
        own[...] = v_own[...]
        far[...] = v_far[...]


def copy_half_body(s, weights, out, sem):
    copy = pltpu.make_async_copy(weights.at[:, 1 - s[2]], out, sem)
    copy.start()
    copy.wait()


def attend_body(s, q, m0, m1, m2, m3, o0, o1, o2, o3, out, scores, top, total, mixed):
    y, zh, core = s[0], s[1], s[2]
    length = q.shape[0]
    half = m0.shape[0] // 2
    me = y * 2 + zh
    rate = 1.0 / math.sqrt(HEAD_DIM) * math.log2(math.e)

    def run(keys, values):
        stacked = jnp.concatenate([q[:, :HEAD_DIM], q[:, HEAD_DIM:]], axis=0)
        blocks = []
        for b in range(4):
            for part in range(2):
                owner = ((y + 4 - b) & 3) * 2 + (zh if part == 0 else 1 - zh)
                blocks.append((b, part, owner))
        for b, part, owner in blocks:
            rows = slice(part * half, (part + 1) * half)
            at = (2 * b + part) * half

            def score(b=b, rows=rows):
                return lax.dot_general(
                    stacked,
                    keys[b][rows, :],
                    (((1,), (1,)), ((), ())),
                    preferred_element_type=f32,
                )

            if b == 0 and part == 0:
                got = score()
                row = lax.broadcasted_iota(jnp.int32, got.shape, 0) & (length - 1)
                col = lax.broadcasted_iota(jnp.int32, got.shape, 1)
                got = jnp.where(col <= row, got, masked_score)
                scores[:, at : at + half] = got
                top[...] = jnp.max(got, axis=1, keepdims=True)
            else:

                @pl.when(owner < me)
                def _(at=at, score=score):
                    got = score()
                    scores[:, at : at + half] = got
                    top[...] = jnp.maximum(top[...], jnp.max(got, axis=1, keepdims=True))

        for b, part, owner in blocks:
            rows = slice(part * half, (part + 1) * half)
            at = (2 * b + part) * half

            def weigh(b=b, rows=rows, at=at):
                weights = jnp.exp2((scores[:, at : at + half] - top[...]) * rate)
                return (
                    jnp.sum(weights, axis=1, keepdims=True),
                    jnp.dot(
                        weights.astype(bf16), values[b][rows, :], preferred_element_type=f32
                    ),
                )

            if b == 0 and part == 0:
                total[...], mixed[...] = weigh()
            else:

                @pl.when(owner < me)
                def _(weigh=weigh):
                    more, product = weigh()
                    total[...] += more
                    mixed[...] += product

        done = (mixed[...] / total[...]).astype(bf16).astype(f32)
        out[:HEAD_DIM, :] = done[:length].T.astype(bf16)
        out[HEAD_DIM:, :] = done[length:].T.astype(bf16)

    @pl.when(core == 0)
    def _():
        run((m0, m1, m2, m3), (o0, o1, o2, o3))

    @pl.when(core != 0)
    def _():
        run((o0, o1, o2, o3), (m0, m1, m2, m3))


def project_body(s, *refs):
    count = (len(refs) - 4) // 2
    own = refs[:count]
    got = refs[count : 2 * count]
    here, there = refs[2 * count : 2 * count + 2]
    outs = refs[2 * count + 2 :]
    each = count // len(outs)
    for i in range(count):
        outs[i // each][(i % each) // 2, i % 2] = (
            jnp.dot(own[i][...], here[...], preferred_element_type=f32)
            + jnp.dot(got[i][...], there[...], preferred_element_type=f32)
        ).astype(bf16)


def add_split_body(s, kept, arrived, *outs):
    rows = kept.shape[0] // len(outs)
    for i, out in enumerate(outs):
        at = slice(i * rows, (i + 1) * rows)
        out[...] = (kept[at].astype(f32) + arrived[at].astype(f32)).astype(bf16)


def running_sums(decay):
    length = decay.shape[0]
    row = lax.broadcasted_iota(jnp.int32, (length, length), 0)
    col = lax.broadcasted_iota(jnp.int32, (length, length), 1)
    lower = (col <= row).astype(f32)
    down = jnp.dot(lower, decay, precision=lax.Precision.HIGHEST, preferred_element_type=f32)
    across = lax.dot_general(
        decay,
        lower,
        (((0,), (1,)), ((), ())),
        precision=lax.Precision.HIGHEST,
        preferred_element_type=f32,
    )
    return down, across


def widen(per_head, width):
    heads = per_head.shape[1]
    row = lax.broadcasted_iota(jnp.int32, (heads, heads * width), 0)
    col = lax.broadcasted_iota(jnp.int32, (heads, heads * width), 1)
    spread = ((col // width) == row).astype(f32)
    return jnp.dot(per_head, spread, precision=lax.Precision.HIGHEST, preferred_element_type=f32)


def closing_body(s, x, in_rows, decay, out):
    heads = decay.shape[1]
    inner = heads * SSM_HEAD_DIM
    length = x.shape[0]
    down, across = running_sums(decay[...])
    tail = widen(jnp.exp(down[length - 1 :, :] - down), SSM_HEAD_DIM)
    scaled = (x[...].astype(f32) * tail).astype(bf16)
    out[:inner, :] = lax.dot_general(
        scaled, in_rows[...], (((0,), (0,)), ((), ())), preferred_element_type=f32
    ).astype(bf16)
    fade = jnp.exp(across[:, length - 1 :])
    fade = jnp.broadcast_to(fade, (heads, N_STATE))
    high = fade.astype(bf16)
    out[inner : inner + 2 * heads, :] = jnp.concatenate(
        [high.astype(f32), fade - high.astype(f32)], axis=0
    ).astype(bf16)


def fades(state, inner, heads):
    both = state[inner : inner + 2 * heads, :].astype(f32)
    return both[:heads] + both[heads:]


def head_rows(h):
    return slice(h * SSM_HEAD_DIM, (h + 1) * SSM_HEAD_DIM)


def pair_body(heads):
    inner = heads * SSM_HEAD_DIM

    def body(s, mine, partner, out):
        def run(first, second):
            fade0 = fades(first, inner, heads)
            fade1 = fades(second, inner, heads)
            for h in range(heads):
                rows = head_rows(h)
                out[rows, :] = (
                    fade1[h : h + 1] * first[rows, :].astype(f32) + second[rows, :].astype(f32)
                ).astype(bf16)
            fade = fade0 * fade1
            high = fade.astype(bf16)
            out[inner : inner + 2 * heads, :] = jnp.concatenate(
                [high.astype(f32), fade - high.astype(f32)], axis=0
            ).astype(bf16)

        @pl.when(s[1] == 0)
        def _():
            run(mine, partner)

        @pl.when(s[1] != 0)
        def _():
            run(partner, mine)

    return body


def scan_body(s, x, in_rows, out_rows, decay, gain, partner, t1, t2, t3, out, entering):
    y, zh = s[0], s[1]
    heads = decay.shape[1]
    inner = heads * SSM_HEAD_DIM
    length = x.shape[0]
    down, across = running_sums(decay[...])
    fade1 = fades(t1, inner, heads)
    fade2 = fades(t2, inner, heads)
    fade0 = fades(partner, inner, heads)
    for h in range(heads):
        rows = head_rows(h)
        third = jnp.where(y >= 3, t3[rows, :].astype(f32), 0.0)
        second = jnp.where(y >= 2, t2[rows, :].astype(f32), 0.0)
        first = jnp.where(y >= 1, t1[rows, :].astype(f32), 0.0)
        state = first + fade1[h : h + 1] * (second + fade2[h : h + 1] * third)
        later = fade0[h : h + 1] * state + partner[rows, :].astype(f32)
        entering[rows, :] = jnp.where(zh == 0, state, later).astype(bf16)
    contract = (((1,), (1,)), ((), ()))
    wide = x[...].astype(f32)
    carried = widen(jnp.exp(down), SSM_HEAD_DIM) * lax.dot_general(
        out_rows[...], entering[...], contract, preferred_element_type=f32
    )
    rest = carried + widen(gain[...], SSM_HEAD_DIM) * wide
    affinity = lax.dot_general(
        out_rows[...], in_rows[...], contract, preferred_element_type=f32
    )
    row = lax.broadcasted_iota(jnp.int32, (length, length), 0)
    col = lax.broadcasted_iota(jnp.int32, (length, length), 1)
    causal = col <= row
    for h in range(heads):
        lanes = slice(h * SSM_HEAD_DIM, (h + 1) * SSM_HEAD_DIM)
        gaps = down[:, h : h + 1] - across[h : h + 1, :]
        mixing = affinity * jnp.exp(jnp.where(causal, gaps, masked_score))
        inside = jnp.dot(mixing.astype(bf16), x[:, lanes], preferred_element_type=f32)
        out[:, lanes] = (inside + rest[:, lanes]).astype(bf16)


def sum_body(count):
    def body(s, *refs):
        total = refs[0][...].astype(f32)
        for ref in refs[1:count]:
            total = total + ref[...].astype(f32)
        refs[count][...] = total.astype(bf16)

    return body


def on_device(
    scan_input,
    input_map,
    output_map,
    log_decay,
    skip_gain,
    query_rows,
    key_rows,
    value_rows,
    out_weight,
):
    section = lax.axis_index("section")
    tp = lax.axis_index("tp")
    y, zh = section // 2, section % 2
    core, chip = tp % 2, tp // 2
    group = tp // (TP // GROUPS)
    shape = jax.ShapeDtypeStruct
    scalars = jnp.stack(
        [y, zh, core, group, group ^ 1] + [chip ^ r for r in range(CHIPS)]
    ).astype(jnp.int32)

    length = query_rows.shape[0]
    head_block = (length, HEAD_DIM)
    own_spec = pl.BlockSpec(head_block, lambda i, s: (0, s[3]))
    far_spec = pl.BlockSpec(head_block, lambda i, s: (0, s[4]))
    block = shape(head_block, bf16)
    own, far = call(
        pick_body,
        scalars,
        [own_spec, own_spec, far_spec, far_spec],
        [block, block],
        (key_rows, value_rows, key_rows, value_rows),
        moved=6 * length * HEAD_DIM * 2,
    )
    pair = jnp.concatenate([own, swap_zh_near(far)], axis=0)

    weights = out_weight.reshape(CHIPS, 2, ROWS, out_weight.shape[1])
    (sent,) = call(
        copy_half_body,
        scalars,
        [pl.BlockSpec(memory_space=pl.ANY)],
        [shape((CHIPS, ROWS, out_weight.shape[1]), bf16)],
        (weights,),
        scratch=[pltpu.SemaphoreType.DMA],
        out_specs=[pl.BlockSpec(memory_space=pl.ANY)],
        moved=4000000,
    )
    got_weight = swap_core(sent.reshape(CHIPS * ROWS, out_weight.shape[1]))

    heads = log_decay.shape[1]
    inner = heads * SSM_HEAD_DIM
    state_shape = shape((inner + 2 * heads, N_STATE), bf16)
    x_spec = whole(scan_input.shape)
    decay_spec = whole(log_decay.shape)
    (closing,) = call(
        closing_body,
        scalars,
        [x_spec, own_spec, decay_spec],
        [state_shape],
        (scan_input, input_map, log_decay),
        flops=2 * length * inner * N_STATE,
        moved=600000,
    )

    pairs = [pair] + [shift_y(pair, d) for d in (1, 2, 3)]
    others = [swap_core(p) for p in pairs]
    (attended,) = call(
        attend_body,
        scalars,
        [whole(query_rows.shape)] + [whole(pair.shape)] * 8,
        [shape(query_rows.shape, bf16)],
        (query_rows, *pairs, *others),
        scratch=[
            pltpu.VMEM((2 * length, 4 * pair.shape[0]), f32),
            pltpu.VMEM((2 * length, 1), f32),
            pltpu.VMEM((2 * length, 1), f32),
            pltpu.VMEM((2 * length, HEAD_DIM), f32),
        ],
        flops=4 * 2 * length * 4 * pair.shape[0] * HEAD_DIM,
        moved=2000000,
    )
    attended_there = swap_core(attended)

    partner = swap_zh(closing)
    (joined,) = call(
        pair_body(heads),
        scalars,
        [whole(closing.shape)] * 2,
        [state_shape],
        (closing, partner),
        moved=400000,
    )
    earlier = [shift_y(joined, d) for d in (1, 2, 3)]

    weight_block = (ROWS, out_weight.shape[1])

    def project(offsets):
        own_specs = [
            pl.BlockSpec(weight_block, lambda i, s, r=r: (s[5 + r] * 2 + s[2], 0)) for r in offsets
        ]
        got_specs = [pl.BlockSpec(weight_block, lambda i, s, r=r: (s[5 + r], 0)) for r in offsets]
        return call(
            project_body,
            scalars,
            own_specs + got_specs + [whole(attended.shape)] * 2,
            [shape((2, 2, ROWS, length), bf16)] * 2,
            [out_weight] * len(offsets)
            + [got_weight] * len(offsets)
            + [attended, attended_there],
            flops=len(offsets) * 2 * ROWS * 512 * length,
            moved=3000000,
        )

    sent1, sent2 = project([4, 5, 8, 9, 14, 15, 10, 11])
    kept1, kept2 = project([0, 1, 12, 13, 2, 3, 6, 7])
    arrived1, arrived2 = swap_x(sent1, 1), swap_x(sent2, 3)

    def add_split(kept, arrived, parts):
        out = shape((kept.shape[0] // parts, *kept.shape[1:]), bf16)
        return call(
            add_split_body,
            scalars,
            [whole(kept.shape)] * 2,
            [out] * parts,
            (kept, arrived),
            moved=6 * kept.size,
        )

    kept1, sent1 = add_split(kept1, arrived1, 2)
    kept2, sent2 = add_split(kept2, arrived2, 2)
    arrived1, arrived2 = swap_x(sent1, 3), swap_x(sent2, 1)
    z0, z1 = add_split(kept1[0], arrived1[0], 2)
    z2, z3 = add_split(kept2[0], arrived2[0], 2)
    arrived = [z0[0]] + [swap_zl(z[0], b) for b, z in ((1, z1), (2, z2), (3, z3))]
    (attn_out,) = call(
        sum_body(4),
        scalars,
        [whole((ROWS, length))] * 4,
        [shape((ROWS, length), bf16)],
        arrived,
        moved=5 * ROWS * length * 2,
    )

    (ssm_out,) = call(
        scan_body,
        scalars,
        [x_spec, own_spec, own_spec, decay_spec, whole((1, heads))]
        + [whole(closing.shape)] * 4,
        [shape(scan_input.shape, bf16)],
        (
            scan_input,
            input_map,
            output_map,
            log_decay,
            skip_gain.reshape(1, heads),
            partner,
            *earlier,
        ),
        scratch=[pltpu.VMEM((inner, N_STATE), bf16)],
        flops=2 * heads * length * length * SSM_HEAD_DIM,
        moved=1500000,
    )
    return (ssm_out, attn_out)


def solution(mesh):
    placed = (
        P("section", "tp"),
        P("section", None),
        P("section", None),
        P("section", "tp"),
        P("tp"),
        P("section", "tp"),
        P("section", None),
        P("section", None),
        P(None, "tp"),
    )
    return jax.shard_map(
        on_device,
        mesh=mesh,
        in_specs=placed,
        out_specs=(P("section", "tp"), P("tp", "section")),
        check_vma=False,
    )
```

```python
import math

import jax
import jax.numpy as jnp
from jax import lax
from jax.experimental import pallas as pl
from jax.experimental.pallas import tpu as pltpu
from jax.sharding import PartitionSpec as P

SCAN_HEADS = 256
SSM_HEAD_DIM = 64
N_STATE = 128
GROUPS = 8
Q_HEADS = 64
KV_HEADS = 8
HEAD_DIM = 128

SECTIONS = 8
TP = 32
ROWS = 256
CHIPS = 16
masked_score = -1e30
bf16 = jnp.bfloat16
f32 = jnp.float32
VMEM_LIMIT = 48 * 1024 * 1024


def swap_core(block):
    return lax.ppermute(block, "tp", [(t, t ^ 1) for t in range(TP)])


def swap_zh(block):
    return lax.ppermute(block, "section", [(s, s ^ 1) for s in range(SECTIONS)])


def shift_y(block, distance):
    route = [(s, (s + 2 * distance) % SECTIONS) for s in range(SECTIONS)]
    return lax.ppermute(block, "section", route)


def swap_zh_near(block):
    route = [
        (s * TP + t, (s ^ 1) * TP + (t ^ 4)) for s in range(SECTIONS) for t in range(TP)
    ]
    return lax.ppermute(block, ("section", "tp"), route)


def swap_x(block, offset):
    return lax.ppermute(block, "tp", [(t, t ^ (8 * offset)) for t in range(TP)])


def swap_x_cross(block, offset):
    return lax.ppermute(block, "tp", [(t, t ^ (8 * offset) ^ 1) for t in range(TP)])


def swap_zl(block, offset):
    return lax.ppermute(block, "tp", [(t, t ^ (2 * offset)) for t in range(TP)])


def params():
    return pltpu.CompilerParams(vmem_limit_bytes=VMEM_LIMIT)


def whole(shape):
    return pl.BlockSpec(shape, lambda i, s: (0,) * len(shape))


def call(body, scalars, in_specs, out_shapes, args, scratch=(), flops=0, moved=0, out_specs=None):
    return pl.pallas_call(
        body,
        grid_spec=pltpu.PrefetchScalarGridSpec(
            num_scalar_prefetch=1,
            grid=(1,),
            in_specs=in_specs,
            out_specs=out_specs or [whole(o.shape) for o in out_shapes],
            scratch_shapes=list(scratch),
        ),
        out_shape=out_shapes,
        compiler_params=params(),
        cost_estimate=pl.CostEstimate(flops=flops, bytes_accessed=moved, transcendentals=0),
    )(scalars, *args)


def pick_body(s, k_own, v_own, k_far, v_far, own, far):
    @pl.when(s[2] == 0)
    def _():
        own[...] = k_own[...]
        far[...] = k_far[...]

    @pl.when(s[2] != 0)
    def _():
        own[...] = v_own[...]
        far[...] = v_far[...]


def copy_blocks_body(offsets):
    def body(s, weights, after, *refs):
        outs, sems = refs[: len(offsets)], refs[len(offsets)]
        copies = []
        for k, (out, blocks) in enumerate(zip(outs, offsets)):
            for i, (r, flip) in enumerate(blocks):
                core = 1 - s[2] if flip else s[2]
                copies.append(
                    pltpu.make_async_copy(
                        weights.at[s[5 + r] * 2 + core], out.at[i], sems.at[len(copies)]
                    )
                )
        for copy in copies:
            copy.start()
        for copy in copies:
            copy.wait()

    return body


def fold(op, block, into=None):
    for at in range(0, block.shape[1], 128):
        part = block[:, at : at + 128]
        into = part if into is None else op(into, part)
    return into


def attend_body(s, q, mine, other, mine_far, other_far, out, scores):
    y, zh, core = s[0], s[1], s[2]
    length = q.shape[0]
    me = y * 2 + zh
    rate = 1.0 / math.sqrt(HEAD_DIM) * math.log2(math.e)

    def run(near_keys, far_keys, near_values, far_values):
        stacked = jnp.concatenate([q[:, :HEAD_DIM], q[:, HEAD_DIM:]], axis=0)
        top = None
        for block in range(8):
            b, part = block // 2, block % 2
            keys, row = (near_keys, block) if b == 0 else (far_keys, block - 2)
            got = lax.dot_general(
                stacked,
                keys[row * length : (row + 1) * length, :],
                (((1,), (1,)), ((), ())),
                preferred_element_type=f32,
            )
            if block == 0:
                row = lax.broadcasted_iota(jnp.int32, got.shape, 0) & (length - 1)
                col = lax.broadcasted_iota(jnp.int32, got.shape, 1)
                got = jnp.where(col <= row, got, masked_score)
            else:
                owner = ((y + 4 - b) & 3) * 2 + (zh if part == 0 else 1 - zh)
                got = got + jnp.where(owner < me, 0.0, masked_score).astype(f32)
            scores[:, block * length : (block + 1) * length] = got
            top = fold(jnp.maximum, got, top)
        top = jnp.max(top, axis=1, keepdims=True) * rate
        total = None
        mixed = jnp.zeros(stacked.shape, f32)
        for b in range(4):
            at = slice(2 * length * b, 2 * length * (b + 1))
            weights = jnp.exp2(scores[:, at] * rate - top)
            total = fold(jnp.add, weights, total)
            value = near_values[...] if b == 0 else far_values[
                2 * length * (b - 1) : 2 * length * b, :
            ]
            mixed = mixed + jnp.dot(weights.astype(bf16), value, preferred_element_type=f32)
        done = mixed / jnp.sum(total, axis=1, keepdims=True)
        done = done.astype(bf16).astype(f32)
        out[:HEAD_DIM, :] = done[:length].T.astype(bf16)
        out[HEAD_DIM:, :] = done[length:].T.astype(bf16)

    @pl.when(core == 0)
    def _():
        run(mine, mine_far, other, other_far)

    @pl.when(core != 0)
    def _():
        run(other, other_far, mine, mine_far)


def project_body(s, own0, own1, own2, own3, mate, s1, x1, s2, x2, a0, ac, a1, a1c, a3, a3c, out1, out2):
    own = (own0, own1, own2, own3)
    here, near = a0[...], ac[...]
    for i in range(4):
        first = i < 2
        same, cross = (s1, x1) if first else (s2, x2)
        there, far = (a1, a1c) if first else (a3, a3c)
        out = out1 if first else out2
        out[i % 2] = (
            jnp.dot(own[i][...], here, preferred_element_type=f32)
            + jnp.dot(mate[i // 2, 0, i % 2], near, preferred_element_type=f32)
            + jnp.dot(same[i % 2], there[...], preferred_element_type=f32)
            + jnp.dot(cross[i % 2], far[...], preferred_element_type=f32)
        ).astype(bf16)


def gather_body(s, *refs):
    rows = refs[0].shape[0]
    for i, ref in enumerate(refs[:-1]):
        refs[-1][i * rows : (i + 1) * rows, :] = ref[...]


def add_split_body(s, kept, arrived, *outs):
    rows = kept.shape[0] // len(outs)
    for i, out in enumerate(outs):
        at = slice(i * rows, (i + 1) * rows)
        out[...] = (kept[at].astype(f32) + arrived[at].astype(f32)).astype(bf16)


def running_sums(decay):
    length = decay.shape[0]
    row = lax.broadcasted_iota(jnp.int32, (length, length), 0)
    col = lax.broadcasted_iota(jnp.int32, (length, length), 1)
    lower = (col <= row).astype(f32)
    down = jnp.dot(lower, decay, precision=lax.Precision.HIGHEST, preferred_element_type=f32)
    across = lax.dot_general(
        decay,
        lower,
        (((0,), (1,)), ((), ())),
        precision=lax.Precision.HIGHEST,
        preferred_element_type=f32,
    )
    return down, across


def widen(per_head, width):
    heads = per_head.shape[1]
    row = lax.broadcasted_iota(jnp.int32, (heads, heads * width), 0)
    col = lax.broadcasted_iota(jnp.int32, (heads, heads * width), 1)
    spread = ((col // width) == row).astype(f32)
    return jnp.dot(per_head, spread, precision=lax.Precision.HIGHEST, preferred_element_type=f32)


def closing_body(s, x, in_rows, decay, out):
    heads = decay.shape[1]
    inner = heads * SSM_HEAD_DIM
    length = x.shape[0]
    down, across = running_sums(decay[...])
    tail = widen(jnp.exp(down[length - 1 :, :] - down), SSM_HEAD_DIM)
    scaled = (x[...].astype(f32) * tail).astype(bf16)
    out[:inner, :] = lax.dot_general(
        scaled, in_rows[...], (((0,), (0,)), ((), ())), preferred_element_type=f32
    ).astype(bf16)
    fade = jnp.exp(across[:, length - 1 :])
    fade = jnp.broadcast_to(fade, (heads, N_STATE))
    high = fade.astype(bf16)
    out[inner : inner + 2 * heads, :] = jnp.concatenate(
        [high.astype(f32), fade - high.astype(f32)], axis=0
    ).astype(bf16)


def fades(state, inner, heads):
    both = state[inner : inner + 2 * heads, :].astype(f32)
    return both[:heads] + both[heads:]


def head_rows(h):
    return slice(h * SSM_HEAD_DIM, (h + 1) * SSM_HEAD_DIM)


def pair_body(heads):
    inner = heads * SSM_HEAD_DIM

    def body(s, mine, partner, out):
        def run(first, second):
            fade0 = fades(first, inner, heads)
            fade1 = fades(second, inner, heads)
            for h in range(heads):
                rows = head_rows(h)
                out[rows, :] = (
                    fade1[h : h + 1] * first[rows, :].astype(f32) + second[rows, :].astype(f32)
                ).astype(bf16)
            fade = fade0 * fade1
            high = fade.astype(bf16)
            out[inner : inner + 2 * heads, :] = jnp.concatenate(
                [high.astype(f32), fade - high.astype(f32)], axis=0
            ).astype(bf16)

        @pl.when(s[1] == 0)
        def _():
            run(mine, partner)

        @pl.when(s[1] != 0)
        def _():
            run(partner, mine)

    return body


def chain_body(heads):
    inner = heads * SSM_HEAD_DIM

    def body(s, joined, near, out):
        fade = fades(joined, inner, heads)
        for h in range(heads):
            rows = head_rows(h)
            before = jnp.where(s[0] >= 1, near[rows, :].astype(f32), 0.0)
            out[rows, :] = (fade[h : h + 1] * before + joined[rows, :].astype(f32)).astype(bf16)

    return body


def scan_body(s, x, in_rows, out_rows, decay, gain, partner, near, far, out, entering):
    y, zh = s[0], s[1]
    heads = decay.shape[1]
    inner = heads * SSM_HEAD_DIM
    length = x.shape[0]
    down, across = running_sums(decay[...])
    fade1 = fades(near, inner, heads)
    fade0 = fades(partner, inner, heads)
    for h in range(heads):
        rows = head_rows(h)
        second = jnp.where(y >= 2, far[rows, :].astype(f32), 0.0)
        first = jnp.where(y >= 1, near[rows, :].astype(f32), 0.0)
        state = first + fade1[h : h + 1] * second
        later = fade0[h : h + 1] * state + partner[rows, :].astype(f32)
        entering[rows, :] = jnp.where(zh == 0, state, later).astype(bf16)
    contract = (((1,), (1,)), ((), ()))
    wide = x[...].astype(f32)
    carried = widen(jnp.exp(down), SSM_HEAD_DIM) * lax.dot_general(
        out_rows[...], entering[...], contract, preferred_element_type=f32
    )
    rest = carried + widen(gain[...], SSM_HEAD_DIM) * wide
    affinity = lax.dot_general(
        out_rows[...], in_rows[...], contract, preferred_element_type=f32
    )
    row = lax.broadcasted_iota(jnp.int32, (length, length), 0)
    col = lax.broadcasted_iota(jnp.int32, (length, length), 1)
    causal = col <= row
    for h in range(heads):
        lanes = slice(h * SSM_HEAD_DIM, (h + 1) * SSM_HEAD_DIM)
        gaps = down[:, h : h + 1] - across[h : h + 1, :]
        mixing = affinity * jnp.exp(jnp.where(causal, gaps, masked_score))
        inside = jnp.dot(mixing.astype(bf16), x[:, lanes], preferred_element_type=f32)
        out[:, lanes] = (inside + rest[:, lanes]).astype(bf16)


def sum_body(count):
    def body(s, *refs):
        total = refs[0][...].astype(f32)
        for ref in refs[1:count]:
            total = total + ref[...].astype(f32)
        refs[count][...] = total.astype(bf16)

    return body


def on_device(
    scan_input,
    input_map,
    output_map,
    log_decay,
    skip_gain,
    query_rows,
    key_rows,
    value_rows,
    out_weight,
):
    section = lax.axis_index("section")
    tp = lax.axis_index("tp")
    y, zh = section // 2, section % 2
    core, chip = tp % 2, tp // 2
    group = tp // (TP // GROUPS)
    shape = jax.ShapeDtypeStruct
    scalars = jnp.stack(
        [y, zh, core, group, group ^ 1] + [chip ^ r for r in range(CHIPS)]
    ).astype(jnp.int32)

    length = query_rows.shape[0]
    head_block = (length, HEAD_DIM)
    own_spec = pl.BlockSpec(head_block, lambda i, s: (0, s[3]))
    far_spec = pl.BlockSpec(head_block, lambda i, s: (0, s[4]))
    block = shape(head_block, bf16)

    def gather(blocks):
        rows, lanes = blocks[0].shape
        (out,) = call(
            gather_body,
            scalars,
            [whole(blocks[0].shape)] * len(blocks),
            [shape((rows * len(blocks), lanes), bf16)],
            blocks,
            moved=4 * len(blocks) * rows * lanes,
        )
        return out

    own, far = call(
        pick_body,
        scalars,
        [own_spec, own_spec, far_spec, far_spec],
        [block, block],
        (key_rows, value_rows, key_rows, value_rows),
        moved=6 * length * HEAD_DIM * 2,
    )
    arrived_far = swap_zh_near(far)

    weights = out_weight.reshape(2 * CHIPS, ROWS, out_weight.shape[1])
    any_spec = pl.BlockSpec(memory_space=pl.ANY)

    def copy_blocks(offsets, after):
        return call(
            copy_blocks_body(offsets),
            scalars,
            [any_spec] * 2,
            [shape((len(o), *weights.shape[1:]), bf16) for o in offsets],
            (weights, after),
            scratch=[pltpu.SemaphoreType.DMA((sum(len(o) for o in offsets),))],
            out_specs=[any_spec] * len(offsets),
            moved=4000000,
        )

    to1, to3 = (4, 5, 8, 9), (14, 15, 10, 11)
    sent = copy_blocks([[(r, flip) for r in to] for to in (to1, to3) for flip in (0, 1)], far)
    same1, cross1 = swap_x(sent[0], 1), swap_x_cross(sent[1], 1)
    same3, cross3 = swap_x(sent[2], 3), swap_x_cross(sent[3], 3)
    (sent_mate,) = copy_blocks([[(r, 1) for r in (0, 1, 12, 13, 2, 3, 6, 7)]], sent[0])
    mate = swap_core(sent_mate)
    pair = gather([own, arrived_far])

    heads = log_decay.shape[1]
    inner = heads * SSM_HEAD_DIM
    state_shape = shape((inner + 2 * heads, N_STATE), bf16)
    x_spec = whole(scan_input.shape)
    decay_spec = whole(log_decay.shape)
    (closing,) = call(
        closing_body,
        scalars,
        [x_spec, own_spec, decay_spec],
        [state_shape],
        (scan_input, input_map, log_decay),
        flops=2 * length * inner * N_STATE,
        moved=600000,
    )

    pair_other = swap_core(pair)
    fetched = gather([shift_y(pair, d) for d in (1, 2, 3)])
    fetched_other = swap_core(fetched)
    (attended,) = call(
        attend_body,
        scalars,
        [whole(query_rows.shape)] + [whole(pair.shape)] * 2 + [whole(fetched.shape)] * 2,
        [shape((query_rows.shape[1], length), bf16)],
        (query_rows, pair, pair_other, fetched, fetched_other),
        scratch=[pltpu.VMEM((2 * length, 4 * pair.shape[0]), f32)],
        flops=4 * 2 * length * 4 * pair.shape[0] * HEAD_DIM,
        moved=2000000,
    )
    attended1, attended3 = swap_x(attended, 1), swap_x(attended, 3)
    heard = [
        attended,
        swap_core(attended),
        attended1,
        swap_core(attended1),
        attended3,
        swap_core(attended3),
    ]

    partner = swap_zh(closing)
    (joined,) = call(
        pair_body(heads),
        scalars,
        [whole(closing.shape)] * 2,
        [state_shape],
        (closing, partner),
        moved=400000,
    )
    near = shift_y(joined, 1)
    (chained,) = call(
        chain_body(heads),
        scalars,
        [whole(closing.shape)] * 2,
        [shape((inner, N_STATE), bf16)],
        (joined, near),
        moved=400000,
    )
    further = shift_y(chained, 2)

    weight_block = (ROWS, out_weight.shape[1])
    part = shape((2, ROWS, length), bf16)

    def project(offsets, half):
        own_specs = [
            pl.BlockSpec(weight_block, lambda i, s, r=r: (s[5 + r] * 2 + s[2], 0)) for r in offsets
        ]
        mate_spec = pl.BlockSpec((2, 1, 2, *weight_block), lambda i, s: (0, half, 0, 0, 0))
        slab_spec = pl.BlockSpec((2, *weight_block), lambda i, s: (half, 0, 0))
        return call(
            project_body,
            scalars,
            own_specs + [mate_spec] + [slab_spec] * 4 + [whole(attended.shape)] * 6,
            [part] * 2,
            [out_weight] * 4
            + [mate.reshape(2, 2, 2, *weight_block), same1, cross1, same3, cross3]
            + heard,
            flops=4 * 2 * ROWS * 1024 * length,
            moved=3000000,
        )

    sent1, sent2 = project([12, 13, 6, 7], 1)
    kept1, kept2 = project([0, 1, 2, 3], 0)
    arrived1, arrived2 = swap_x(sent1, 3), swap_x(sent2, 1)

    def add_split(kept, arrived):
        out = shape((1, ROWS, length), bf16)
        return call(
            add_split_body,
            scalars,
            [whole(kept.shape)] * 2,
            [out] * 2,
            (kept, arrived),
            moved=6 * kept.size,
        )

    z0, z1 = add_split(kept1, arrived1)
    z2, z3 = add_split(kept2, arrived2)
    arrived = [z0[0]] + [swap_zl(z[0], b) for b, z in ((2, z2), (3, z3), (1, z1))]
    (attn_out,) = call(
        sum_body(4),
        scalars,
        [whole((ROWS, length))] * 4,
        [shape((ROWS, length), bf16)],
        arrived,
        moved=5 * ROWS * length * 2,
    )

    (ssm_out,) = call(
        scan_body,
        scalars,
        [x_spec, own_spec, own_spec, decay_spec, whole((1, heads))]
        + [whole(closing.shape)] * 2
        + [whole(further.shape)],
        [shape(scan_input.shape, bf16)],
        (
            scan_input,
            input_map,
            output_map,
            log_decay,
            skip_gain.reshape(1, heads),
            partner,
            near,
            further,
        ),
        scratch=[pltpu.VMEM((inner, N_STATE), bf16)],
        flops=2 * heads * length * length * SSM_HEAD_DIM,
        moved=1500000,
    )
    return (ssm_out, attn_out)


def solution(mesh):
    placed = (
        P("section", "tp"),
        P("section", None),
        P("section", None),
        P("section", "tp"),
        P("tp"),
        P("section", "tp"),
        P("section", None),
        P("section", None),
        P(None, "tp"),
    )
    return jax.shard_map(
        on_device,
        mesh=mesh,
        in_specs=placed,
        out_specs=(P("section", "tp"), P("tp", "section")),
        check_vma=False,
    )
```

```python
import math

import jax
import jax.numpy as jnp
from jax import lax
from jax.experimental import pallas as pl
from jax.experimental.pallas import tpu as pltpu
from jax.sharding import PartitionSpec as P

SCAN_HEADS = 256
SSM_HEAD_DIM = 64
N_STATE = 128
GROUPS = 8
Q_HEADS = 64
KV_HEADS = 8
HEAD_DIM = 128

SECTIONS = 8
TP = 32
ROWS = 256
CHIPS = 16
masked_score = -1e30
bf16 = jnp.bfloat16
f32 = jnp.float32


def swap_core(block):
    return lax.ppermute(block, "tp", [(t, t ^ 1) for t in range(TP)])


def swap_zh(block):
    return lax.ppermute(block, "section", [(s, s ^ 1) for s in range(SECTIONS)])


def shift_y(block, distance):
    route = [(s, (s + 2 * distance) % SECTIONS) for s in range(SECTIONS)]
    return lax.ppermute(block, "section", route)


def swap_zh_near(block):
    route = [
        (s * TP + t, (s ^ 1) * TP + (t ^ 4)) for s in range(SECTIONS) for t in range(TP)
    ]
    return lax.ppermute(block, ("section", "tp"), route)


def swap_x(block, offset):
    return lax.ppermute(block, "tp", [(t, t ^ (8 * offset)) for t in range(TP)])


def swap_zl(block, offset):
    return lax.ppermute(block, "tp", [(t, t ^ (2 * offset)) for t in range(TP)])


def whole(shape):
    return pl.BlockSpec(shape, lambda i, s: (0,) * len(shape))


def call(
    body, scalars, in_specs, out_shapes, args, scratch=(), limit=16, after=(), us=0.5, out_specs=None
):
    first, count = 1 + len(in_specs), len(after)

    def ordered(*refs):
        body(*refs[:first], *refs[first + count :])

    return pl.pallas_call(
        ordered,
        grid_spec=pltpu.PrefetchScalarGridSpec(
            num_scalar_prefetch=1,
            grid=(1,),
            in_specs=list(in_specs) + [pl.BlockSpec(memory_space=pl.ANY)] * count,
            out_specs=out_specs or [whole(o.shape) for o in out_shapes],
            scratch_shapes=list(scratch),
        ),
        out_shape=out_shapes,
        compiler_params=pltpu.CompilerParams(vmem_limit_bytes=limit * 1024 * 1024),
        cost_estimate=pl.CostEstimate(
            flops=int(us * 1e9), bytes_accessed=int(us * 3.5e6), transcendentals=0
        ),
    )(scalars, *args, *after)


def copy_body(s, weights, mate, own, sems):
    copies = [
        pltpu.make_async_copy(weights.at[:, 1 - s[2]], mate, sems.at[0]),
        pltpu.make_async_copy(weights.at[:, s[2]], own, sems.at[1]),
    ]
    for copy in copies:
        copy.start()
    for copy in copies:
        copy.wait()


def join_body(s, *refs):
    rows = refs[0].shape[0]
    for i, ref in enumerate(refs[:-1]):
        refs[-1][i * rows : (i + 1) * rows, :] = ref[...]


def fold(op, block, into=None):
    for at in range(0, block.shape[1], 128):
        part = block[:, at : at + 128]
        into = part if into is None else op(into, part)
    return into


def attend(s, q, keys, values, first, scores):
    y, zh = s[0], s[1]
    length = q.shape[0]
    me = y * 2 + zh
    rate = 1.0 / math.sqrt(HEAD_DIM) * math.log2(math.e)
    stacked = jnp.concatenate([q[:, :HEAD_DIM], q[:, HEAD_DIM:]], axis=0)
    top = None
    for b, key in enumerate(keys):
        for part in range(2):
            got = lax.dot_general(
                stacked,
                key[part * length : (part + 1) * length, :],
                (((1,), (1,)), ((), ())),
                preferred_element_type=f32,
            )
            if first + b == 0 and part == 0:
                row = lax.broadcasted_iota(jnp.int32, got.shape, 0) & (length - 1)
                col = lax.broadcasted_iota(jnp.int32, got.shape, 1)
                got = jnp.where(col <= row, got, masked_score)
            else:
                owner = ((y + 4 - first - b) & 3) * 2 + (zh if part == 0 else 1 - zh)
                got = got + jnp.where(owner < me, 0.0, masked_score).astype(f32)
            scores[:, (2 * b + part) * length : (2 * b + part + 1) * length] = got
            top = fold(jnp.maximum, got, top)
    top = jnp.max(top, axis=1, keepdims=True) * rate
    total = None
    mixed = jnp.zeros(stacked.shape, f32)
    for b, value in enumerate(values):
        weights = jnp.exp2(scores[:, 2 * length * b : 2 * length * (b + 1)] * rate - top)
        total = fold(jnp.add, weights, total)
        mixed = mixed + jnp.dot(weights.astype(bf16), value[...], preferred_element_type=f32)
    return top, total, mixed


def attend_near_body(s, q, mine, other, tops, totals, mixeds, scores):
    def run(keys, values):
        top, total, mixed = attend(s, q, [keys], [values], 0, scores)
        tops[...] = jnp.broadcast_to(top, tops.shape)
        totals[...] = total
        mixeds[...] = mixed

    @pl.when(s[2] == 0)
    def _():
        run(mine, other)

    @pl.when(s[2] != 0)
    def _():
        run(other, mine)


def attend_far_body(s, q, mine, other, tops, totals, mixeds, out, scores):
    length = q.shape[0]

    def run(keys, values):
        parts = [slice(2 * length * b, 2 * length * (b + 1)) for b in range(3)]
        far_top, far_total, far_mixed = attend(
            s, q, [keys[at, :] for at in parts], [values[at, :] for at in parts], 1, scores
        )
        near_top = tops[...][:, :1]
        top = jnp.maximum(near_top, far_top)
        near, far = jnp.exp2(near_top - top), jnp.exp2(far_top - top)
        total = jnp.sum(totals[...] * near + far_total * far, axis=1, keepdims=True)
        done = (mixeds[...] * near + far_mixed * far) / total
        out[:HEAD_DIM, :] = done[:length].T.astype(bf16)
        out[HEAD_DIM:, :] = done[length:].T.astype(bf16)

    @pl.when(s[2] == 0)
    def _():
        run(mine, other)

    @pl.when(s[2] != 0)
    def _():
        run(other, mine)


def project_body(s, *refs):
    count = (len(refs) - 4) // 2
    own = refs[:count]
    got = refs[count : 2 * count]
    here, there = refs[2 * count : 2 * count + 2]
    outs = refs[2 * count + 2 :]
    each = count // len(outs)
    for i in range(count):
        outs[i // each][(i % each) // 2, i % 2] = (
            jnp.dot(own[i][0], here[...], preferred_element_type=f32)
            + jnp.dot(got[i][0], there[...], preferred_element_type=f32)
        ).astype(bf16)


def add_split_body(s, kept, arrived, *outs):
    rows = kept.shape[0] // len(outs)
    for i, out in enumerate(outs):
        at = slice(i * rows, (i + 1) * rows)
        out[...] = (kept[at].astype(f32) + arrived[at].astype(f32)).astype(bf16)


def running_sums(decay):
    length = decay.shape[0]
    row = lax.broadcasted_iota(jnp.int32, (length, length), 0)
    col = lax.broadcasted_iota(jnp.int32, (length, length), 1)
    lower = (col <= row).astype(f32)
    down = jnp.dot(lower, decay, precision=lax.Precision.HIGHEST, preferred_element_type=f32)
    across = lax.dot_general(
        decay,
        lower,
        (((0,), (1,)), ((), ())),
        precision=lax.Precision.HIGHEST,
        preferred_element_type=f32,
    )
    return down, across


def widen(per_head, width):
    heads = per_head.shape[1]
    row = lax.broadcasted_iota(jnp.int32, (heads, heads * width), 0)
    col = lax.broadcasted_iota(jnp.int32, (heads, heads * width), 1)
    spread = ((col // width) == row).astype(f32)
    return jnp.dot(per_head, spread, precision=lax.Precision.HIGHEST, preferred_element_type=f32)


def closing_body(s, x, in_rows, decay, out):
    heads = decay.shape[1]
    inner = heads * SSM_HEAD_DIM
    length = x.shape[0]
    down, across = running_sums(decay[...])
    tail = widen(jnp.exp(down[length - 1 :, :] - down), SSM_HEAD_DIM)
    scaled = (x[...].astype(f32) * tail).astype(bf16)
    out[:inner, :] = lax.dot_general(
        scaled, in_rows[...], (((0,), (0,)), ((), ())), preferred_element_type=f32
    ).astype(bf16)
    fade = jnp.exp(across[:, length - 1 :])
    fade = jnp.broadcast_to(fade, (heads, N_STATE))
    high = fade.astype(bf16)
    out[inner : inner + 2 * heads, :] = jnp.concatenate(
        [high.astype(f32), fade - high.astype(f32)], axis=0
    ).astype(bf16)


def fades(state, inner, heads):
    both = state[inner : inner + 2 * heads, :].astype(f32)
    return both[:heads] + both[heads:]


def head_rows(h):
    return slice(h * SSM_HEAD_DIM, (h + 1) * SSM_HEAD_DIM)


def pair_body(heads):
    inner = heads * SSM_HEAD_DIM

    def body(s, mine, partner, out):
        def run(first, second):
            fade0 = fades(first, inner, heads)
            fade1 = fades(second, inner, heads)
            for h in range(heads):
                rows = head_rows(h)
                out[rows, :] = (
                    fade1[h : h + 1] * first[rows, :].astype(f32) + second[rows, :].astype(f32)
                ).astype(bf16)
            fade = fade0 * fade1
            high = fade.astype(bf16)
            out[inner : inner + 2 * heads, :] = jnp.concatenate(
                [high.astype(f32), fade - high.astype(f32)], axis=0
            ).astype(bf16)

        @pl.when(s[1] == 0)
        def _():
            run(mine, partner)

        @pl.when(s[1] != 0)
        def _():
            run(partner, mine)

    return body


def chain_body(heads):
    inner = heads * SSM_HEAD_DIM

    def body(s, joined, near, out):
        fade = fades(joined, inner, heads)
        for h in range(heads):
            rows = head_rows(h)
            before = jnp.where(s[0] >= 1, near[rows, :].astype(f32), 0.0)
            out[rows, :] = (fade[h : h + 1] * before + joined[rows, :].astype(f32)).astype(bf16)

    return body


def scan_body(s, x, in_rows, out_rows, decay, gain, partner, near, far, out, entering):
    y, zh = s[0], s[1]
    heads = decay.shape[1]
    inner = heads * SSM_HEAD_DIM
    length = x.shape[0]
    down, across = running_sums(decay[...])
    fade1 = fades(near, inner, heads)
    fade0 = fades(partner, inner, heads)
    for h in range(heads):
        rows = head_rows(h)
        second = jnp.where(y >= 2, far[rows, :].astype(f32), 0.0)
        first = jnp.where(y >= 1, near[rows, :].astype(f32), 0.0)
        state = first + fade1[h : h + 1] * second
        later = fade0[h : h + 1] * state + partner[rows, :].astype(f32)
        entering[rows, :] = jnp.where(zh == 0, state, later).astype(bf16)
    contract = (((1,), (1,)), ((), ()))
    wide = x[...].astype(f32)
    carried = widen(jnp.exp(down), SSM_HEAD_DIM) * lax.dot_general(
        out_rows[...], entering[...], contract, preferred_element_type=f32
    )
    rest = carried + widen(gain[...], SSM_HEAD_DIM) * wide
    affinity = lax.dot_general(
        out_rows[...], in_rows[...], contract, preferred_element_type=f32
    )
    row = lax.broadcasted_iota(jnp.int32, (length, length), 0)
    col = lax.broadcasted_iota(jnp.int32, (length, length), 1)
    causal = col <= row
    for h in range(heads):
        lanes = slice(h * SSM_HEAD_DIM, (h + 1) * SSM_HEAD_DIM)
        gaps = down[:, h : h + 1] - across[h : h + 1, :]
        mixing = affinity * jnp.exp(jnp.where(causal, gaps, masked_score))
        inside = jnp.dot(mixing.astype(bf16), x[:, lanes], preferred_element_type=f32)
        out[:, lanes] = (inside + rest[:, lanes]).astype(bf16)


def sum_body(count):
    def body(s, *refs):
        total = refs[0][...].astype(f32)
        for ref in refs[1:count]:
            total = total + ref[...].astype(f32)
        refs[count][...] = total.astype(bf16)

    return body


def on_device(
    scan_input,
    input_map,
    output_map,
    log_decay,
    skip_gain,
    query_rows,
    key_rows,
    value_rows,
    out_weight,
):
    section = lax.axis_index("section")
    tp = lax.axis_index("tp")
    y, zh = section // 2, section % 2
    core, chip = tp % 2, tp // 2
    group = tp // (TP // GROUPS)
    shape = jax.ShapeDtypeStruct
    scalars = jnp.stack(
        [y, zh, core, group, group ^ 1] + [chip ^ r for r in range(CHIPS)]
    ).astype(jnp.int32)

    length = query_rows.shape[0]
    head_block = (length, HEAD_DIM)

    def columns(array, index):
        return lax.dynamic_slice_in_dim(array, index * HEAD_DIM, HEAD_DIM, 1)

    first = core == 0
    sent = jnp.where(first, columns(key_rows, group ^ 1), columns(value_rows, group ^ 1))
    arrived_pair = swap_zh_near(sent)
    own = jnp.where(first, columns(key_rows, group), columns(value_rows, group))
    in_rows, out_rows = columns(input_map, group), columns(output_map, group)

    (pair,) = call(
        join_body,
        scalars,
        [whole(head_block)] * 2,
        [shape((2 * length, HEAD_DIM), bf16)],
        (own, arrived_pair),
    )
    fetched = [shift_y(pair, d) for d in (2, 1, 3)]
    pair_other = swap_core(pair)

    weight_block = (ROWS, out_weight.shape[1])
    sent_mate, own_weight = call(
        copy_body,
        scalars,
        [pl.BlockSpec(memory_space=pl.ANY)],
        [shape((CHIPS, *weight_block), bf16)] * 2,
        [out_weight.reshape(CHIPS, 2, *weight_block)],
        scratch=[pltpu.SemaphoreType.DMA((2,))],
        out_specs=[pl.BlockSpec(memory_space=pl.ANY)] * 2,
        after=[sent],
    )
    mate = swap_core(sent_mate)
    heads = log_decay.shape[1]
    inner = heads * SSM_HEAD_DIM
    state_shape = shape((inner + 2 * heads, N_STATE), bf16)
    x_spec = whole(scan_input.shape)
    decay_spec = whole(log_decay.shape)
    (closing,) = call(
        closing_body,
        scalars,
        [x_spec, whole(head_block), decay_spec],
        [state_shape],
        (scan_input, in_rows, log_decay),
        us=2,
    )

    stat = shape((2 * length, HEAD_DIM), f32)
    q_spec = whole(query_rows.shape)
    near_part = call(
        attend_near_body,
        scalars,
        [q_spec] + [whole(pair.shape)] * 2,
        [stat] * 3,
        (query_rows, pair, pair_other),
        scratch=[pltpu.VMEM((2 * length, 2 * length), f32)],
        us=2.2,
    )
    (others,) = call(
        join_body,
        scalars,
        [whole(pair.shape)] * 3,
        [shape((6 * length, HEAD_DIM), bf16)],
        (fetched[1], fetched[0], fetched[2]),
        after=[closing, near_part[0]],
    )
    others_there = swap_core(others)
    (attended,) = call(
        attend_far_body,
        scalars,
        [q_spec] + [whole(others.shape)] * 2 + [whole(stat.shape)] * 3,
        [shape((query_rows.shape[1], length), bf16)],
        (query_rows, others, others_there, *near_part),
        scratch=[pltpu.VMEM((2 * length, 6 * length), f32)],
        us=40,
    )
    attended_there = swap_core(attended)

    partner = swap_zh(closing)
    def project(offsets, after=()):
        return call(
            project_body,
            scalars,
            [
                pl.BlockSpec((1, *weight_block), lambda i, s, r=r: (s[5 + r], 0, 0))
                for r in offsets * 2
            ]
            + [whole(attended.shape)] * 2,
            [shape((2, 2, ROWS, length), bf16)] * 2,
            [own_weight] * len(offsets)
            + [mate] * len(offsets)
            + [attended, attended_there],
            after=after,
            us=1.3,
        )

    sent1, sent2 = project([4, 5, 8, 9, 14, 15, 10, 11])
    (joined,) = call(
        pair_body(heads),
        scalars,
        [whole(closing.shape)] * 2,
        [state_shape],
        (closing, partner),
        after=[sent1],
    )
    near = shift_y(joined, 1)
    (chained,) = call(
        chain_body(heads),
        scalars,
        [whole(closing.shape)] * 2,
        [shape((inner, N_STATE), bf16)],
        (joined, near),
    )
    further = shift_y(chained, 2)

    kept1, kept2 = project([0, 1, 12, 13, 2, 3, 6, 7], [sent1])
    arrived1, arrived2 = swap_x(sent1, 1), swap_x(sent2, 3)

    def add_split(kept, arrived, after=()):
        out = shape((kept.shape[0] // 2, *kept.shape[1:]), bf16)
        return call(add_split_body, scalars, [whole(kept.shape)] * 2, [out] * 2, (kept, arrived), after=after)

    kept1, sent1 = add_split(kept1, arrived1, [joined])
    kept2, sent2 = add_split(kept2, arrived2)
    arrived1, arrived2 = swap_x(sent1, 3), swap_x(sent2, 1)
    z0, z1 = add_split(kept1[0], arrived1[0], [chained])
    z2, z3 = add_split(kept2[0], arrived2[0])
    arrived = [z0[0]] + [swap_zl(z[0], b) for b, z in ((2, z2), (3, z3), (1, z1))]
    (attn_out,) = call(
        sum_body(4),
        scalars,
        [whole((ROWS, length))] * 4,
        [shape((ROWS, length), bf16)],
        arrived,
        us=1.3,
    )

    (ssm_out,) = call(
        scan_body,
        scalars,
        [x_spec, whole(head_block), whole(head_block), decay_spec, whole((1, heads))]
        + [whole(closing.shape)] * 2
        + [whole(further.shape)],
        [shape(scan_input.shape, bf16)],
        (
            scan_input,
            in_rows,
            out_rows,
            log_decay,
            skip_gain.reshape(1, heads),
            partner,
            near,
            further,
        ),
        scratch=[pltpu.VMEM((inner, N_STATE), bf16)],
        us=3,
    )
    return (ssm_out, attn_out)


def solution(mesh):
    placed = (
        P("section", "tp"),
        P("section", None),
        P("section", None),
        P("section", "tp"),
        P("tp"),
        P("section", "tp"),
        P("section", None),
        P("section", None),
        P(None, "tp"),
    )
    return jax.shard_map(
        on_device,
        mesh=mesh,
        in_specs=placed,
        out_specs=(P("section", "tp"), P("tp", "section")),
        check_vma=False,
    )
```

```python
import math

import jax
import jax.numpy as jnp
from jax import lax
from jax.experimental import pallas as pl
from jax.experimental.pallas import tpu as pltpu
from jax.sharding import PartitionSpec as P

SCAN_HEADS = 256
SSM_HEAD_DIM = 64
N_STATE = 128
GROUPS = 8
Q_HEADS = 64
KV_HEADS = 8
HEAD_DIM = 128

SECTIONS = 8
TP = 32
ROWS = 256
CHIPS = 16
masked_score = -1e30
bf16 = jnp.bfloat16
f32 = jnp.float32


def swap_core(block):
    return lax.ppermute(block, "tp", [(t, t ^ 1) for t in range(TP)])


def swap_zh(block):
    return lax.ppermute(block, "section", [(s, s ^ 1) for s in range(SECTIONS)])


def shift_y(block, distance):
    route = [(s, (s + 2 * distance) % SECTIONS) for s in range(SECTIONS)]
    return lax.ppermute(block, "section", route)


def swap_zh_near(block):
    route = [
        (s * TP + t, (s ^ 1) * TP + (t ^ 4)) for s in range(SECTIONS) for t in range(TP)
    ]
    return lax.ppermute(block, ("section", "tp"), route)


def swap_x(block, offset):
    return lax.ppermute(block, "tp", [(t, t ^ (8 * offset)) for t in range(TP)])


def swap_zl(block, offset):
    return lax.ppermute(block, "tp", [(t, t ^ (2 * offset)) for t in range(TP)])


def whole(shape):
    return pl.BlockSpec(shape, lambda i, s: (0,) * len(shape))


def call(
    body, scalars, in_specs, out_shapes, args, scratch=(), limit=16, after=(), us=0.5, out_specs=None
):
    first, count = 1 + len(in_specs), len(after)

    def ordered(*refs):
        body(*refs[:first], *refs[first + count :])

    return pl.pallas_call(
        ordered,
        grid_spec=pltpu.PrefetchScalarGridSpec(
            num_scalar_prefetch=1,
            grid=(1,),
            in_specs=list(in_specs) + [pl.BlockSpec(memory_space=pl.ANY)] * count,
            out_specs=out_specs or [whole(o.shape) for o in out_shapes],
            scratch_shapes=list(scratch),
        ),
        out_shape=out_shapes,
        compiler_params=pltpu.CompilerParams(vmem_limit_bytes=limit * 1024 * 1024),
        cost_estimate=pl.CostEstimate(
            flops=int(us * 1e9), bytes_accessed=int(us * 3.5e6), transcendentals=0
        ),
    )(scalars, *args, *after)


def copy_body(s, weights, mate, own, sems):
    copies = [
        pltpu.make_async_copy(weights.at[:, 1 - s[2]], mate, sems.at[0]),
        pltpu.make_async_copy(weights.at[:, s[2]], own, sems.at[1]),
    ]
    for copy in copies:
        copy.start()
    for copy in copies:
        copy.wait()


def join_body(s, *refs):
    at = 0
    for ref in refs[:-1]:
        refs[-1][at : at + ref.shape[0], :] = ref[...]
        at += ref.shape[0]


def fold(op, block, into=None):
    for at in range(0, block.shape[1], 128):
        part = block[:, at : at + 128]
        into = part if into is None else op(into, part)
    return into


def attend(s, q, keys, values, owners, scores):
    length = q.shape[0]
    me = s[0] * 2 + s[1]
    rate = 1.0 / math.sqrt(HEAD_DIM) * math.log2(math.e)
    stacked = jnp.concatenate([q[:, :HEAD_DIM], q[:, HEAD_DIM:]], axis=0)
    top = None
    for b, owner in enumerate(owners):
        at = slice(b * length, (b + 1) * length)
        got = lax.dot_general(
            stacked, keys[at, :], (((1,), (1,)), ((), ())), preferred_element_type=f32
        )
        if owner is None:
            row = lax.broadcasted_iota(jnp.int32, got.shape, 0) & (length - 1)
            col = lax.broadcasted_iota(jnp.int32, got.shape, 1)
            got = jnp.where(col <= row, got, masked_score)
        else:
            got = got + jnp.where(owner < me, 0.0, masked_score).astype(f32)
        scores[:, at] = got
        top = fold(jnp.maximum, got, top)
    top = jnp.max(top, axis=1, keepdims=True) * rate
    total = None
    mixed = jnp.zeros(stacked.shape, f32)
    for b in range(len(owners)):
        at = slice(b * length, (b + 1) * length)
        weights = jnp.exp2(scores[:, at] * rate - top)
        total = fold(jnp.add, weights, total)
        mixed = mixed + jnp.dot(
            weights.astype(bf16), values[at, :], preferred_element_type=f32
        )
    return top, total, mixed


def attend_near_body(s, q, keys, values, tops, totals, mixeds, scores):
    top, total, mixed = attend(s, q, keys, values, [None], scores)
    tops[...] = jnp.broadcast_to(top, tops.shape)
    totals[...] = total
    mixeds[...] = mixed


def attend_far_body(s, q, mine, other, tops, totals, mixeds, out, scores):
    y, zh = s[0], s[1]
    length = q.shape[0]
    owners = [y * 2 + 1 - zh]
    for b in range(1, 4):
        there = ((y + 4 - b) & 3) * 2
        owners += [there + zh, there + 1 - zh]

    def run(keys, values):
        far_top, far_total, far_mixed = attend(s, q, keys, values, owners, scores)
        near_top = tops[...][:, :1]
        top = jnp.maximum(near_top, far_top)
        near, far = jnp.exp2(near_top - top), jnp.exp2(far_top - top)
        total = jnp.sum(totals[...] * near + far_total * far, axis=1, keepdims=True)
        done = (mixeds[...] * near + far_mixed * far) / total
        out[:HEAD_DIM, :] = done[:length].T.astype(bf16)
        out[HEAD_DIM:, :] = done[length:].T.astype(bf16)

    @pl.when(s[2] == 0)
    def _():
        run(mine, other)

    @pl.when(s[2] != 0)
    def _():
        run(other, mine)


def project_body(s, *refs):
    count = (len(refs) - 4) // 2
    own = refs[:count]
    got = refs[count : 2 * count]
    here, there = refs[2 * count : 2 * count + 2]
    outs = refs[2 * count + 2 :]
    each = count // len(outs)
    for i in range(count):
        outs[i // each][(i % each) // 2, i % 2] = (
            jnp.dot(own[i][0], here[...], preferred_element_type=f32)
            + jnp.dot(got[i][0], there[...], preferred_element_type=f32)
        ).astype(bf16)


def add_split_body(s, kept, arrived, *outs):
    rows = kept.shape[0] // len(outs)
    for i, out in enumerate(outs):
        at = slice(i * rows, (i + 1) * rows)
        out[...] = (kept[at].astype(f32) + arrived[at].astype(f32)).astype(bf16)


def running_sums(decay):
    length = decay.shape[0]
    row = lax.broadcasted_iota(jnp.int32, (length, length), 0)
    col = lax.broadcasted_iota(jnp.int32, (length, length), 1)
    lower = (col <= row).astype(f32)
    down = jnp.dot(lower, decay, precision=lax.Precision.HIGHEST, preferred_element_type=f32)
    across = lax.dot_general(
        decay,
        lower,
        (((0,), (1,)), ((), ())),
        precision=lax.Precision.HIGHEST,
        preferred_element_type=f32,
    )
    return down, across


def widen(per_head, width):
    heads = per_head.shape[1]
    row = lax.broadcasted_iota(jnp.int32, (heads, heads * width), 0)
    col = lax.broadcasted_iota(jnp.int32, (heads, heads * width), 1)
    spread = ((col // width) == row).astype(f32)
    return jnp.dot(per_head, spread, precision=lax.Precision.HIGHEST, preferred_element_type=f32)


def closing_body(s, x, in_rows, decay, out):
    heads = decay.shape[1]
    inner = heads * SSM_HEAD_DIM
    length = x.shape[0]
    down, across = running_sums(decay[...])
    tail = widen(jnp.exp(down[length - 1 :, :] - down), SSM_HEAD_DIM)
    scaled = (x[...].astype(f32) * tail).astype(bf16)
    out[:inner, :] = lax.dot_general(
        scaled, in_rows[...], (((0,), (0,)), ((), ())), preferred_element_type=f32
    ).astype(bf16)
    fade = jnp.exp(across[:, length - 1 :])
    fade = jnp.broadcast_to(fade, (heads, N_STATE))
    high = fade.astype(bf16)
    out[inner : inner + 2 * heads, :] = jnp.concatenate(
        [high.astype(f32), fade - high.astype(f32)], axis=0
    ).astype(bf16)


def fades(state, inner, heads):
    both = state[inner : inner + 2 * heads, :].astype(f32)
    return both[:heads] + both[heads:]


def head_rows(h):
    return slice(h * SSM_HEAD_DIM, (h + 1) * SSM_HEAD_DIM)


def pair_body(heads):
    inner = heads * SSM_HEAD_DIM

    def body(s, mine, partner, out):
        def run(first, second):
            fade0 = fades(first, inner, heads)
            fade1 = fades(second, inner, heads)
            for h in range(heads):
                rows = head_rows(h)
                out[rows, :] = (
                    fade1[h : h + 1] * first[rows, :].astype(f32) + second[rows, :].astype(f32)
                ).astype(bf16)
            fade = fade0 * fade1
            high = fade.astype(bf16)
            out[inner : inner + 2 * heads, :] = jnp.concatenate(
                [high.astype(f32), fade - high.astype(f32)], axis=0
            ).astype(bf16)

        @pl.when(s[1] == 0)
        def _():
            run(mine, partner)

        @pl.when(s[1] != 0)
        def _():
            run(partner, mine)

    return body


def chain_body(heads):
    inner = heads * SSM_HEAD_DIM

    def body(s, joined, near, out):
        fade = fades(joined, inner, heads)
        for h in range(heads):
            rows = head_rows(h)
            before = jnp.where(s[0] >= 1, near[rows, :].astype(f32), 0.0)
            out[rows, :] = (fade[h : h + 1] * before + joined[rows, :].astype(f32)).astype(bf16)

    return body


def scan_body(s, x, in_rows, out_rows, decay, gain, partner, near, far, out, entering):
    y, zh = s[0], s[1]
    heads = decay.shape[1]
    inner = heads * SSM_HEAD_DIM
    length = x.shape[0]
    down, across = running_sums(decay[...])
    fade1 = fades(near, inner, heads)
    fade0 = fades(partner, inner, heads)
    for h in range(heads):
        rows = head_rows(h)
        second = jnp.where(y >= 2, far[rows, :].astype(f32), 0.0)
        first = jnp.where(y >= 1, near[rows, :].astype(f32), 0.0)
        state = first + fade1[h : h + 1] * second
        later = fade0[h : h + 1] * state + partner[rows, :].astype(f32)
        entering[rows, :] = jnp.where(zh == 0, state, later).astype(bf16)
    contract = (((1,), (1,)), ((), ()))
    wide = x[...].astype(f32)
    carried = widen(jnp.exp(down), SSM_HEAD_DIM) * lax.dot_general(
        out_rows[...], entering[...], contract, preferred_element_type=f32
    )
    rest = carried + widen(gain[...], SSM_HEAD_DIM) * wide
    affinity = lax.dot_general(
        out_rows[...], in_rows[...], contract, preferred_element_type=f32
    )
    row = lax.broadcasted_iota(jnp.int32, (length, length), 0)
    col = lax.broadcasted_iota(jnp.int32, (length, length), 1)
    causal = col <= row
    for h in range(heads):
        lanes = slice(h * SSM_HEAD_DIM, (h + 1) * SSM_HEAD_DIM)
        gaps = down[:, h : h + 1] - across[h : h + 1, :]
        mixing = affinity * jnp.exp(jnp.where(causal, gaps, masked_score))
        inside = jnp.dot(mixing.astype(bf16), x[:, lanes], preferred_element_type=f32)
        out[:, lanes] = (inside + rest[:, lanes]).astype(bf16)


def sum_body(count):
    def body(s, *refs):
        total = refs[0][...].astype(f32)
        for ref in refs[1:count]:
            total = total + ref[...].astype(f32)
        refs[count][...] = total.astype(bf16)

    return body


def on_device(
    scan_input,
    input_map,
    output_map,
    log_decay,
    skip_gain,
    query_rows,
    key_rows,
    value_rows,
    out_weight,
):
    section = lax.axis_index("section")
    tp = lax.axis_index("tp")
    y, zh = section // 2, section % 2
    core, chip = tp % 2, tp // 2
    group = tp // (TP // GROUPS)
    shape = jax.ShapeDtypeStruct
    scalars = jnp.stack(
        [y, zh, core, group, group ^ 1] + [chip ^ r for r in range(CHIPS)]
    ).astype(jnp.int32)

    length = query_rows.shape[0]
    head_block = (length, HEAD_DIM)

    def columns(array, index):
        return lax.dynamic_slice_in_dim(array, index * HEAD_DIM, HEAD_DIM, 1)

    first = core == 0
    sent = jnp.where(first, columns(key_rows, group ^ 1), columns(value_rows, group ^ 1))
    arrived_pair = swap_zh_near(sent)
    own_keys, own_values = columns(key_rows, group), columns(value_rows, group)
    own = jnp.where(first, own_keys, own_values)
    in_rows, out_rows = columns(input_map, group), columns(output_map, group)

    (pair,) = call(
        join_body,
        scalars,
        [whole(head_block)] * 2,
        [shape((2 * length, HEAD_DIM), bf16)],
        (own, arrived_pair),
    )
    fetched = [shift_y(pair, d) for d in (2, 1, 3)]

    weight_block = (ROWS, out_weight.shape[1])
    sent_mate, own_weight = call(
        copy_body,
        scalars,
        [pl.BlockSpec(memory_space=pl.ANY)],
        [shape((CHIPS, *weight_block), bf16)] * 2,
        [out_weight.reshape(CHIPS, 2, *weight_block)],
        scratch=[pltpu.SemaphoreType.DMA((2,))],
        out_specs=[pl.BlockSpec(memory_space=pl.ANY)] * 2,
        after=[sent],
    )
    mate = swap_core(sent_mate)
    heads = log_decay.shape[1]
    inner = heads * SSM_HEAD_DIM
    state_shape = shape((inner + 2 * heads, N_STATE), bf16)
    x_spec = whole(scan_input.shape)
    decay_spec = whole(log_decay.shape)
    (closing,) = call(
        closing_body,
        scalars,
        [x_spec, whole(head_block), decay_spec],
        [state_shape],
        (scan_input, in_rows, log_decay),
        us=0.3,
    )

    stat = shape((2 * length, HEAD_DIM), f32)
    q_spec = whole(query_rows.shape)
    near_part = call(
        attend_near_body,
        scalars,
        [q_spec] + [whole(head_block)] * 2,
        [stat] * 3,
        (query_rows, own_keys, own_values),
        scratch=[pltpu.VMEM((2 * length, length), f32)],
        us=0.3,
    )
    (others,) = call(
        join_body,
        scalars,
        [whole(head_block)] + [whole(pair.shape)] * 3,
        [shape((7 * length, HEAD_DIM), bf16)],
        (arrived_pair, fetched[1], fetched[0], fetched[2]),
        after=[closing, near_part[0]],
    )
    others_there = swap_core(others)
    (attended,) = call(
        attend_far_body,
        scalars,
        [q_spec] + [whole(others.shape)] * 2 + [whole(stat.shape)] * 3,
        [shape((query_rows.shape[1], length), bf16)],
        (query_rows, others, others_there, *near_part),
        scratch=[pltpu.VMEM((2 * length, 7 * length), f32)],
        us=40,
    )
    attended_there = swap_core(attended)

    partner = swap_zh(closing)
    def project(offsets, after=()):
        return call(
            project_body,
            scalars,
            [
                pl.BlockSpec((1, *weight_block), lambda i, s, r=r: (s[5 + r], 0, 0))
                for r in offsets * 2
            ]
            + [whole(attended.shape)] * 2,
            [shape((2, 2, ROWS, length), bf16)] * 2,
            [own_weight] * len(offsets)
            + [mate] * len(offsets)
            + [attended, attended_there],
            after=after,
            us=1.3,
        )

    sent1, sent2 = project([4, 5, 8, 9, 14, 15, 10, 11])
    (joined,) = call(
        pair_body(heads),
        scalars,
        [whole(closing.shape)] * 2,
        [state_shape],
        (closing, partner),
        after=[sent1],
    )
    near = shift_y(joined, 1)
    (chained,) = call(
        chain_body(heads),
        scalars,
        [whole(closing.shape)] * 2,
        [shape((inner, N_STATE), bf16)],
        (joined, near),
    )
    further = shift_y(chained, 2)

    kept1, kept2 = project([0, 1, 12, 13, 2, 3, 6, 7], [sent1])
    arrived1, arrived2 = swap_x(sent1, 1), swap_x(sent2, 3)

    def add_split(kept, arrived, after=()):
        out = shape((kept.shape[0] // 2, *kept.shape[1:]), bf16)
        return call(add_split_body, scalars, [whole(kept.shape)] * 2, [out] * 2, (kept, arrived), after=after)

    kept1, sent1 = add_split(kept1, arrived1, [joined])
    kept2, sent2 = add_split(kept2, arrived2)
    arrived1, arrived2 = swap_x(sent1, 3), swap_x(sent2, 1)
    z0, z1 = add_split(kept1[0], arrived1[0], [chained])
    z2, z3 = add_split(kept2[0], arrived2[0])
    arrived = [z0[0]] + [swap_zl(z[0], b) for b, z in ((2, z2), (3, z3), (1, z1))]
    (attn_out,) = call(
        sum_body(4),
        scalars,
        [whole((ROWS, length))] * 4,
        [shape((ROWS, length), bf16)],
        arrived,
        us=1.3,
    )

    (ssm_out,) = call(
        scan_body,
        scalars,
        [x_spec, whole(head_block), whole(head_block), decay_spec, whole((1, heads))]
        + [whole(closing.shape)] * 2
        + [whole(further.shape)],
        [shape(scan_input.shape, bf16)],
        (
            scan_input,
            in_rows,
            out_rows,
            log_decay,
            skip_gain.reshape(1, heads),
            partner,
            near,
            further,
        ),
        scratch=[pltpu.VMEM((inner, N_STATE), bf16)],
        us=3,
    )
    return (ssm_out, attn_out)


def solution(mesh):
    placed = (
        P("section", "tp"),
        P("section", None),
        P("section", None),
        P("section", "tp"),
        P("tp"),
        P("section", "tp"),
        P("section", None),
        P("section", None),
        P(None, "tp"),
    )
    return jax.shard_map(
        on_device,
        mesh=mesh,
        in_specs=placed,
        out_specs=(P("section", "tp"), P("tp", "section")),
        check_vma=False,
    )
```

```python
import math

import jax
import jax.numpy as jnp
from jax import lax
from jax.experimental import pallas as pl
from jax.experimental.pallas import tpu as pltpu
from jax.sharding import PartitionSpec as P

SCAN_HEADS = 256
SSM_HEAD_DIM = 64
N_STATE = 128
GROUPS = 8
Q_HEADS = 64
KV_HEADS = 8
HEAD_DIM = 128

SECTIONS = 8
TP = 32
ROWS = 256
CHIPS = 16
masked_score = -1e30
bf16 = jnp.bfloat16
f32 = jnp.float32


def swap_core(block):
    return lax.ppermute(block, "tp", [(t, t ^ 1) for t in range(TP)])


def swap_zh(block):
    return lax.ppermute(block, "section", [(s, s ^ 1) for s in range(SECTIONS)])


def shift_y(block, distance):
    route = [(s, (s + 2 * distance) % SECTIONS) for s in range(SECTIONS)]
    return lax.ppermute(block, "section", route)


def swap_zh_near(block):
    route = [
        (s * TP + t, (s ^ 1) * TP + (t ^ 4)) for s in range(SECTIONS) for t in range(TP)
    ]
    return lax.ppermute(block, ("section", "tp"), route)


def swap_x(block, offset):
    return lax.ppermute(block, "tp", [(t, t ^ (8 * offset)) for t in range(TP)])


def swap_zl(block, offset):
    return lax.ppermute(block, "tp", [(t, t ^ (2 * offset)) for t in range(TP)])


def whole(shape):
    return pl.BlockSpec(shape, lambda i, s: (0,) * len(shape))


def call(
    body, scalars, in_specs, out_shapes, args, scratch=(), limit=16, after=(), us=0.5, out_specs=None
):
    first, count = 1 + len(in_specs), len(after)

    def ordered(*refs):
        body(*refs[:first], *refs[first + count :])

    return pl.pallas_call(
        ordered,
        grid_spec=pltpu.PrefetchScalarGridSpec(
            num_scalar_prefetch=1,
            grid=(1,),
            in_specs=list(in_specs) + [pl.BlockSpec(memory_space=pl.ANY)] * count,
            out_specs=out_specs or [whole(o.shape) for o in out_shapes],
            scratch_shapes=list(scratch),
        ),
        out_shape=out_shapes,
        compiler_params=pltpu.CompilerParams(vmem_limit_bytes=limit * 1024 * 1024),
        cost_estimate=pl.CostEstimate(
            flops=int(us * 1e9), bytes_accessed=int(us * 3.5e6), transcendentals=0
        ),
    )(scalars, *args, *after)


def copy_body(s, weights, mate, own, sems):
    copies = [
        pltpu.make_async_copy(weights.at[:, 1 - s[2]], mate, sems.at[0]),
        pltpu.make_async_copy(weights.at[:, s[2]], own, sems.at[1]),
    ]
    for copy in copies:
        copy.start()
    for copy in copies:
        copy.wait()


def join_body(s, *refs):
    at = 0
    for ref in refs[:-1]:
        refs[-1][at : at + ref.shape[0], :] = ref[...]
        at += ref.shape[0]


def fold(op, block, into=None):
    for at in range(0, block.shape[1], 128):
        part = block[:, at : at + 128]
        into = part if into is None else op(into, part)
    return into


def attend(s, q, keys, values, owners, scores):
    length = q.shape[0]
    me = s[0] * 2 + s[1]
    rate = 1.0 / math.sqrt(HEAD_DIM) * math.log2(math.e)
    stacked = jnp.concatenate([q[:, :HEAD_DIM], q[:, HEAD_DIM:]], axis=0)
    top = None
    for b, owner in enumerate(owners):
        at = slice(b * length, (b + 1) * length)
        got = lax.dot_general(
            stacked, keys[at, :], (((1,), (1,)), ((), ())), preferred_element_type=f32
        )
        if owner is None:
            row = lax.broadcasted_iota(jnp.int32, got.shape, 0) & (length - 1)
            col = lax.broadcasted_iota(jnp.int32, got.shape, 1)
            got = jnp.where(col <= row, got, masked_score)
        elif not isinstance(owner, int):
            got = got + jnp.where(owner < me, 0.0, masked_score).astype(f32)
        scores[:, at] = got
        top = fold(jnp.maximum, got, top)
    top = jnp.max(top, axis=1, keepdims=True) * rate
    total = None
    mixed = jnp.zeros(stacked.shape, f32)
    for b in range(len(owners)):
        at = slice(b * length, (b + 1) * length)
        weights = jnp.exp2(scores[:, at] * rate - top)
        total = fold(jnp.add, weights, total)
        mixed = mixed + jnp.dot(
            weights.astype(bf16), values[at, :], preferred_element_type=f32
        )
    return top, total, mixed


def attend_near_body(s, q, keys, values, tops, totals, mixeds, scores):
    top, total, mixed = attend(s, q, keys, values, [None], scores)
    tops[...] = jnp.broadcast_to(top, tops.shape)
    totals[...] = total
    mixeds[...] = mixed


def attend_far_body(s, q, mine, other, tops, totals, mixeds, out, scores):
    y, zh = s[0], s[1]
    length = q.shape[0]

    def run(keys, values, count):
        owners = [y * 2 + 1 - zh] + [-1] * (count - 1)
        far_top, far_total, far_mixed = attend(s, q, keys, values, owners, scores)
        near_top = tops[...][:, :1]
        top = jnp.maximum(near_top, far_top)
        near, far = jnp.exp2(near_top - top), jnp.exp2(far_top - top)
        total = jnp.sum(totals[...] * near + far_total * far, axis=1, keepdims=True)
        done = (mixeds[...] * near + far_mixed * far) / total
        out[:HEAD_DIM, :] = done[:length].T.astype(bf16)
        out[HEAD_DIM:, :] = done[length:].T.astype(bf16)

    for rank in range(SECTIONS // 2):
        for core in range(2):

            @pl.when((y == rank) & (s[2] == core))
            def _(rank=rank, core=core):
                keys, values = (mine, other) if core == 0 else (other, mine)
                run(keys, values, 1 + 2 * rank)


def project_body(s, *refs):
    count = (len(refs) - 4) // 2
    own = refs[:count]
    got = refs[count : 2 * count]
    here, there = refs[2 * count : 2 * count + 2]
    outs = refs[2 * count + 2 :]
    each = count // len(outs)
    for i in range(count):
        outs[i // each][(i % each) // 2, i % 2] = (
            jnp.dot(own[i][0], here[...], preferred_element_type=f32)
            + jnp.dot(got[i][0], there[...], preferred_element_type=f32)
        ).astype(bf16)


def add_split_body(s, kept, arrived, *outs):
    rows = kept.shape[0] // len(outs)
    for i, out in enumerate(outs):
        at = slice(i * rows, (i + 1) * rows)
        out[...] = (kept[at].astype(f32) + arrived[at].astype(f32)).astype(bf16)


def running_sums(decay):
    length = decay.shape[0]
    row = lax.broadcasted_iota(jnp.int32, (length, length), 0)
    col = lax.broadcasted_iota(jnp.int32, (length, length), 1)
    lower = (col <= row).astype(f32)
    down = jnp.dot(lower, decay, precision=lax.Precision.HIGHEST, preferred_element_type=f32)
    across = lax.dot_general(
        decay,
        lower,
        (((0,), (1,)), ((), ())),
        precision=lax.Precision.HIGHEST,
        preferred_element_type=f32,
    )
    return down, across


def widen(per_head, width):
    heads = per_head.shape[1]
    row = lax.broadcasted_iota(jnp.int32, (heads, heads * width), 0)
    col = lax.broadcasted_iota(jnp.int32, (heads, heads * width), 1)
    spread = ((col // width) == row).astype(f32)
    return jnp.dot(per_head, spread, precision=lax.Precision.HIGHEST, preferred_element_type=f32)


def closing_body(s, x, in_rows, decay, out):
    heads = decay.shape[1]
    inner = heads * SSM_HEAD_DIM
    length = x.shape[0]
    down, across = running_sums(decay[...])
    tail = widen(jnp.exp(down[length - 1 :, :] - down), SSM_HEAD_DIM)
    scaled = (x[...].astype(f32) * tail).astype(bf16)
    out[:inner, :] = lax.dot_general(
        scaled, in_rows[...], (((0,), (0,)), ((), ())), preferred_element_type=f32
    ).astype(bf16)
    fade = jnp.exp(across[:, length - 1 :])
    fade = jnp.broadcast_to(fade, (heads, N_STATE))
    high = fade.astype(bf16)
    out[inner : inner + 2 * heads, :] = jnp.concatenate(
        [high.astype(f32), fade - high.astype(f32)], axis=0
    ).astype(bf16)


def fades(state, inner, heads):
    both = state[inner : inner + 2 * heads, :].astype(f32)
    return both[:heads] + both[heads:]


def head_rows(h):
    return slice(h * SSM_HEAD_DIM, (h + 1) * SSM_HEAD_DIM)


def pair_body(heads):
    inner = heads * SSM_HEAD_DIM

    def body(s, mine, partner, out):
        def run(first, second):
            fade0 = fades(first, inner, heads)
            fade1 = fades(second, inner, heads)
            for h in range(heads):
                rows = head_rows(h)
                out[rows, :] = (
                    fade1[h : h + 1] * first[rows, :].astype(f32) + second[rows, :].astype(f32)
                ).astype(bf16)
            fade = fade0 * fade1
            high = fade.astype(bf16)
            out[inner : inner + 2 * heads, :] = jnp.concatenate(
                [high.astype(f32), fade - high.astype(f32)], axis=0
            ).astype(bf16)

        @pl.when(s[1] == 0)
        def _():
            run(mine, partner)

        @pl.when(s[1] != 0)
        def _():
            run(partner, mine)

    return body


def scan_body(s, x, in_rows, out_rows, decay, gain, partner, t1, t2, t3, out, entering):
    y, zh = s[0], s[1]
    heads = decay.shape[1]
    inner = heads * SSM_HEAD_DIM
    length = x.shape[0]
    down, across = running_sums(decay[...])
    fade1 = fades(t1, inner, heads)
    fade2 = fades(t2, inner, heads)
    fade0 = fades(partner, inner, heads)
    for h in range(heads):
        rows = head_rows(h)
        third = jnp.where(y >= 3, t3[rows, :].astype(f32), 0.0)
        second = jnp.where(y >= 2, t2[rows, :].astype(f32), 0.0)
        first = jnp.where(y >= 1, t1[rows, :].astype(f32), 0.0)
        state = first + fade1[h : h + 1] * (second + fade2[h : h + 1] * third)
        later = fade0[h : h + 1] * state + partner[rows, :].astype(f32)
        entering[rows, :] = jnp.where(zh == 0, state, later).astype(bf16)
    contract = (((1,), (1,)), ((), ()))
    wide = x[...].astype(f32)
    carried = widen(jnp.exp(down), SSM_HEAD_DIM) * lax.dot_general(
        out_rows[...], entering[...], contract, preferred_element_type=f32
    )
    rest = carried + widen(gain[...], SSM_HEAD_DIM) * wide
    affinity = lax.dot_general(
        out_rows[...], in_rows[...], contract, preferred_element_type=f32
    )
    row = lax.broadcasted_iota(jnp.int32, (length, length), 0)
    col = lax.broadcasted_iota(jnp.int32, (length, length), 1)
    causal = col <= row
    for h in range(heads):
        lanes = slice(h * SSM_HEAD_DIM, (h + 1) * SSM_HEAD_DIM)
        gaps = down[:, h : h + 1] - across[h : h + 1, :]
        mixing = affinity * jnp.exp(jnp.where(causal, gaps, masked_score))
        inside = jnp.dot(mixing.astype(bf16), x[:, lanes], preferred_element_type=f32)
        out[:, lanes] = (inside + rest[:, lanes]).astype(bf16)


def sum_body(count):
    def body(s, *refs):
        total = refs[0][...].astype(f32)
        for ref in refs[1:count]:
            total = total + ref[...].astype(f32)
        refs[count][...] = total.astype(bf16)

    return body


def on_device(
    scan_input,
    input_map,
    output_map,
    log_decay,
    skip_gain,
    query_rows,
    key_rows,
    value_rows,
    out_weight,
):
    section = lax.axis_index("section")
    tp = lax.axis_index("tp")
    y, zh = section // 2, section % 2
    core, chip = tp % 2, tp // 2
    group = tp // (TP // GROUPS)
    shape = jax.ShapeDtypeStruct
    scalars = jnp.stack(
        [y, zh, core, group, group ^ 1] + [chip ^ r for r in range(CHIPS)]
    ).astype(jnp.int32)

    length = query_rows.shape[0]
    head_block = (length, HEAD_DIM)

    def columns(array, index):
        return lax.dynamic_slice_in_dim(array, index * HEAD_DIM, HEAD_DIM, 1)

    first = core == 0
    sent = jnp.where(first, columns(key_rows, group ^ 1), columns(value_rows, group ^ 1))
    arrived_pair = swap_zh_near(sent)
    own_keys, own_values = columns(key_rows, group), columns(value_rows, group)
    own = jnp.where(first, own_keys, own_values)
    in_rows, out_rows = columns(input_map, group), columns(output_map, group)

    (pair,) = call(
        join_body,
        scalars,
        [whole(head_block)] * 2,
        [shape((2 * length, HEAD_DIM), bf16)],
        (own, arrived_pair),
    )
    fetched = [shift_y(pair, d) for d in (2, 1, 3)]

    weight_block = (ROWS, out_weight.shape[1])
    sent_mate, own_weight = call(
        copy_body,
        scalars,
        [pl.BlockSpec(memory_space=pl.ANY)],
        [shape((CHIPS, *weight_block), bf16)] * 2,
        [out_weight.reshape(CHIPS, 2, *weight_block)],
        scratch=[pltpu.SemaphoreType.DMA((2,))],
        out_specs=[pl.BlockSpec(memory_space=pl.ANY)] * 2,
        after=[sent],
    )
    mate = swap_core(sent_mate)
    heads = log_decay.shape[1]
    inner = heads * SSM_HEAD_DIM
    state_shape = shape((inner + 2 * heads, N_STATE), bf16)
    x_spec = whole(scan_input.shape)
    decay_spec = whole(log_decay.shape)
    (closing,) = call(
        closing_body,
        scalars,
        [x_spec, whole(head_block), decay_spec],
        [state_shape],
        (scan_input, in_rows, log_decay),
        us=0.3,
    )

    stat = shape((2 * length, HEAD_DIM), f32)
    q_spec = whole(query_rows.shape)
    near_part = call(
        attend_near_body,
        scalars,
        [q_spec] + [whole(head_block)] * 2,
        [stat] * 3,
        (query_rows, own_keys, own_values),
        scratch=[pltpu.VMEM((2 * length, length), f32)],
        us=0.3,
    )
    (others,) = call(
        join_body,
        scalars,
        [whole(head_block)] + [whole(pair.shape)] * 3,
        [shape((7 * length, HEAD_DIM), bf16)],
        (arrived_pair, fetched[1], fetched[0], fetched[2]),
        after=[closing, near_part[0]],
    )
    others_there = swap_core(others)
    (attended,) = call(
        attend_far_body,
        scalars,
        [q_spec] + [whole(others.shape)] * 2 + [whole(stat.shape)] * 3,
        [shape((query_rows.shape[1], length), bf16)],
        (query_rows, others, others_there, *near_part),
        scratch=[pltpu.VMEM((2 * length, 7 * length), f32)],
        us=40,
    )
    attended_there = swap_core(attended)

    partner = swap_zh(closing)
    def project(offsets, after=()):
        return call(
            project_body,
            scalars,
            [
                pl.BlockSpec((1, *weight_block), lambda i, s, r=r: (s[5 + r], 0, 0))
                for r in offsets * 2
            ]
            + [whole(attended.shape)] * 2,
            [shape((2, 2, ROWS, length), bf16)] * 2,
            [own_weight] * len(offsets)
            + [mate] * len(offsets)
            + [attended, attended_there],
            after=after,
            us=1.3,
        )

    sent1, sent2 = project([4, 5, 8, 9, 14, 15, 10, 11])
    kept1, kept2 = project([0, 1, 12, 13, 2, 3, 6, 7], [sent1])
    arrived1, arrived2 = swap_x(sent1, 1), swap_x(sent2, 3)

    def add_split(kept, arrived):
        out = shape((kept.shape[0] // 2, *kept.shape[1:]), bf16)
        return call(add_split_body, scalars, [whole(kept.shape)] * 2, [out] * 2, (kept, arrived))

    kept1, sent1 = add_split(kept1, arrived1)
    kept2, sent2 = add_split(kept2, arrived2)
    arrived1, arrived2 = swap_x(sent1, 3), swap_x(sent2, 1)
    (joined,) = call(
        pair_body(heads),
        scalars,
        [whole(closing.shape)] * 2,
        [state_shape],
        (closing, partner),
        after=[sent1, sent2],
    )
    earlier = [shift_y(joined, d) for d in (2, 1, 3)]
    z0, z1 = add_split(kept1[0], arrived1[0])
    z2, z3 = add_split(kept2[0], arrived2[0])
    arrived = [z0[0]] + [swap_zl(z[0], b) for b, z in ((2, z2), (3, z3), (1, z1))]
    (attn_out,) = call(
        sum_body(4),
        scalars,
        [whole((ROWS, length))] * 4,
        [shape((ROWS, length), bf16)],
        arrived,
        us=1.3,
    )

    (ssm_out,) = call(
        scan_body,
        scalars,
        [x_spec, whole(head_block), whole(head_block), decay_spec, whole((1, heads))]
        + [whole(closing.shape)] * 4,
        [shape(scan_input.shape, bf16)],
        (
            scan_input,
            in_rows,
            out_rows,
            log_decay,
            skip_gain.reshape(1, heads),
            partner,
            earlier[1],
            earlier[0],
            earlier[2],
        ),
        scratch=[pltpu.VMEM((inner, N_STATE), bf16)],
        after=[z1, z3],
        us=3,
    )
    return (ssm_out, attn_out)


def solution(mesh):
    placed = (
        P("section", "tp"),
        P("section", None),
        P("section", None),
        P("section", "tp"),
        P("tp"),
        P("section", "tp"),
        P("section", None),
        P("section", None),
        P(None, "tp"),
    )
    return jax.shard_map(
        on_device,
        mesh=mesh,
        in_specs=placed,
        out_specs=(P("section", "tp"), P("tp", "section")),
        check_vma=False,
    )
```

```python
import math

import jax
import jax.numpy as jnp
from jax import lax
from jax.experimental import pallas as pl
from jax.experimental.pallas import tpu as pltpu
from jax.sharding import PartitionSpec as P

SCAN_HEADS = 256
SSM_HEAD_DIM = 64
N_STATE = 128
GROUPS = 8
Q_HEADS = 64
KV_HEADS = 8
HEAD_DIM = 128

SECTIONS = 8
TP = 32
ROWS = 256
CHIPS = 16
masked_score = -1e30
bf16 = jnp.bfloat16
f32 = jnp.float32


def swap_core(block):
    return lax.ppermute(block, "tp", [(t, t ^ 1) for t in range(TP)])


def swap_zh(block):
    return lax.ppermute(block, "section", [(s, s ^ 1) for s in range(SECTIONS)])


def shift_y(block, distance):
    route = [(s, (s + 2 * distance) % SECTIONS) for s in range(SECTIONS)]
    return lax.ppermute(block, "section", route)


def swap_zh_near(block):
    route = [
        (s * TP + t, (s ^ 1) * TP + (t ^ 4)) for s in range(SECTIONS) for t in range(TP)
    ]
    return lax.ppermute(block, ("section", "tp"), route)


def swap_x(block, offset):
    return lax.ppermute(block, "tp", [(t, t ^ (8 * offset)) for t in range(TP)])


def swap_zl(block, offset):
    return lax.ppermute(block, "tp", [(t, t ^ (2 * offset)) for t in range(TP)])


def whole(shape):
    return pl.BlockSpec(memory_space=pltpu.VMEM)


class Place:
    def __getitem__(self, item):
        if item < 2:
            section = lax.axis_index("section")
            return section >> 1 if item == 0 else section & 1
        tp = lax.axis_index("tp")
        return tp & 1 if item == 2 else (tp >> 1) ^ (item - 5)


def call(
    body, in_specs, out_shapes, args, scratch=(), limit=16, after=(), us=0.5, out_specs=None
):
    first, count = len(in_specs), len(after)

    def ordered(*refs):
        body(Place(), *refs[:first], *refs[first + count :])

    return pl.pallas_call(
        ordered,
        in_specs=list(in_specs) + [pl.BlockSpec(memory_space=pl.ANY)] * count,
        out_specs=out_specs or [whole(o.shape) for o in out_shapes],
        scratch_shapes=list(scratch),
        out_shape=out_shapes,
        compiler_params=pltpu.CompilerParams(vmem_limit_bytes=limit * 1024 * 1024),
        cost_estimate=pl.CostEstimate(
            flops=int(us * 1e9), bytes_accessed=int(us * 3.5e6), transcendentals=0
        ),
    )(*args, *after)


def copy_body(s, weights, mate, own, sems):
    copies = [
        pltpu.make_async_copy(weights.at[:, 1 - s[2]], mate, sems.at[0]),
        pltpu.make_async_copy(weights.at[:, s[2]], own, sems.at[1]),
    ]
    for copy in copies:
        copy.start()
    for copy in copies:
        copy.wait()


def join_body(s, *refs):
    at = 0
    for ref in refs[:-1]:
        refs[-1][at : at + ref.shape[0], :] = ref[...]
        at += ref.shape[0]


def fold(op, block, into=None):
    for at in range(0, block.shape[1], 128):
        part = block[:, at : at + 128]
        into = part if into is None else op(into, part)
    return into


def attend(s, q, keys, values, owners, scores):
    length = q.shape[0]
    me = s[0] * 2 + s[1]
    rate = 1.0 / math.sqrt(HEAD_DIM) * math.log2(math.e)
    stacked = jnp.concatenate([q[:, :HEAD_DIM], q[:, HEAD_DIM:]], axis=0)
    top = None
    for b, owner in enumerate(owners):
        at = slice(b * length, (b + 1) * length)
        got = lax.dot_general(
            stacked, keys[at, :], (((1,), (1,)), ((), ())), preferred_element_type=f32
        )
        if owner is None:
            row = lax.broadcasted_iota(jnp.int32, got.shape, 0) & (length - 1)
            col = lax.broadcasted_iota(jnp.int32, got.shape, 1)
            got = jnp.where(col <= row, got, masked_score)
        elif not isinstance(owner, int):
            got = got + jnp.where(owner < me, 0.0, masked_score).astype(f32)
        scores[:, at] = got
        top = fold(jnp.maximum, got, top)
    top = jnp.max(top, axis=1, keepdims=True) * rate
    total = None
    mixed = jnp.zeros(stacked.shape, f32)
    for b in range(len(owners)):
        at = slice(b * length, (b + 1) * length)
        weights = jnp.exp2(scores[:, at] * rate - top)
        total = fold(jnp.add, weights, total)
        mixed = mixed + jnp.dot(
            weights.astype(bf16), values[at, :], preferred_element_type=f32
        )
    return top, total, mixed


def attend_near_body(s, q, keys, values, tops, totals, mixeds, scores):
    top, total, mixed = attend(s, q, keys, values, [None], scores)
    tops[...] = jnp.broadcast_to(top, tops.shape)
    totals[...] = total
    mixeds[...] = mixed


def attend_far_body(s, q, mine, other, tops, totals, mixeds, out, scores):
    y, zh = s[0], s[1]
    length = q.shape[0]

    def run(keys, values, count):
        owners = [y * 2 + 1 - zh] + [-1] * (count - 1)
        far_top, far_total, far_mixed = attend(s, q, keys, values, owners, scores)
        near_top = tops[...][:, :1]
        top = jnp.maximum(near_top, far_top)
        near, far = jnp.exp2(near_top - top), jnp.exp2(far_top - top)
        total = jnp.sum(totals[...] * near + far_total * far, axis=1, keepdims=True)
        done = (mixeds[...] * near + far_mixed * far) / total
        out[:HEAD_DIM, :] = done[:length].T.astype(bf16)
        out[HEAD_DIM:, :] = done[length:].T.astype(bf16)

    for rank in range(SECTIONS // 2):
        for core in range(2):

            @pl.when((y == rank) & (s[2] == core))
            def _(rank=rank, core=core):
                keys, values = (mine, other) if core == 0 else (other, mine)
                run(keys, values, 1 + 2 * rank)


def project_body(offsets):
    def body(s, own, mate, here, there, *outs):
        each = len(offsets) // len(outs)
        for i, r in enumerate(offsets):
            outs[i // each][(i % each) // 2, i % 2] = (
                jnp.dot(own[s[5 + r]], here[...], preferred_element_type=f32)
                + jnp.dot(mate[s[5 + r]], there[...], preferred_element_type=f32)
            ).astype(bf16)

    return body


def add_split_body(s, kept1, arrived1, kept2, arrived2, *outs):
    half = len(outs) // 2
    for kept, arrived, pieces in (
        (kept1, arrived1, outs[:half]),
        (kept2, arrived2, outs[half:]),
    ):
        for i, out in enumerate(pieces):
            out[...] = (kept[i].astype(f32) + arrived[i].astype(f32)).astype(bf16)


def running_sums(decay):
    length = decay.shape[0]
    row = lax.broadcasted_iota(jnp.int32, (length, length), 0)
    col = lax.broadcasted_iota(jnp.int32, (length, length), 1)
    lower = (col <= row).astype(f32)
    down = jnp.dot(lower, decay, precision=lax.Precision.HIGHEST, preferred_element_type=f32)
    across = lax.dot_general(
        decay,
        lower,
        (((0,), (1,)), ((), ())),
        precision=lax.Precision.HIGHEST,
        preferred_element_type=f32,
    )
    return down, across


def widen(per_head, width):
    heads = per_head.shape[1]
    row = lax.broadcasted_iota(jnp.int32, (heads, heads * width), 0)
    col = lax.broadcasted_iota(jnp.int32, (heads, heads * width), 1)
    spread = ((col // width) == row).astype(f32)
    return jnp.dot(per_head, spread, precision=lax.Precision.HIGHEST, preferred_element_type=f32)


def closing_body(s, x, in_rows, decay, out):
    heads = decay.shape[1]
    inner = heads * SSM_HEAD_DIM
    length = x.shape[0]
    down, across = running_sums(decay[...])
    tail = widen(jnp.exp(down[length - 1 :, :] - down), SSM_HEAD_DIM)
    scaled = (x[...].astype(f32) * tail).astype(bf16)
    out[:inner, :] = lax.dot_general(
        scaled, in_rows[...], (((0,), (0,)), ((), ())), preferred_element_type=f32
    ).astype(bf16)
    fade = jnp.exp(across[:, length - 1 :])
    fade = jnp.broadcast_to(fade, (heads, N_STATE))
    high = fade.astype(bf16)
    out[inner : inner + 2 * heads, :] = jnp.concatenate(
        [high.astype(f32), fade - high.astype(f32)], axis=0
    ).astype(bf16)


def fades(state, inner, heads):
    both = state[inner : inner + 2 * heads, :].astype(f32)
    return both[:heads] + both[heads:]


def head_rows(h):
    return slice(h * SSM_HEAD_DIM, (h + 1) * SSM_HEAD_DIM)


def pair_body(heads):
    inner = heads * SSM_HEAD_DIM

    def body(s, mine, partner, out):
        def run(first, second):
            fade0 = fades(first, inner, heads)
            fade1 = fades(second, inner, heads)
            for h in range(heads):
                rows = head_rows(h)
                out[rows, :] = (
                    fade1[h : h + 1] * first[rows, :].astype(f32) + second[rows, :].astype(f32)
                ).astype(bf16)
            fade = fade0 * fade1
            high = fade.astype(bf16)
            out[inner : inner + 2 * heads, :] = jnp.concatenate(
                [high.astype(f32), fade - high.astype(f32)], axis=0
            ).astype(bf16)

        @pl.when(s[1] == 0)
        def _():
            run(mine, partner)

        @pl.when(s[1] != 0)
        def _():
            run(partner, mine)

    return body


def scan_body(s, x, in_rows, out_rows, decay, gain, partner, t1, t2, t3, out, entering):
    y, zh = s[0], s[1]
    heads = decay.shape[1]
    inner = heads * SSM_HEAD_DIM
    length = x.shape[0]
    down, across = running_sums(decay[...])
    fade1 = fades(t1, inner, heads)
    fade2 = fades(t2, inner, heads)
    fade0 = fades(partner, inner, heads)
    for h in range(heads):
        rows = head_rows(h)
        third = jnp.where(y >= 3, t3[rows, :].astype(f32), 0.0)
        second = jnp.where(y >= 2, t2[rows, :].astype(f32), 0.0)
        first = jnp.where(y >= 1, t1[rows, :].astype(f32), 0.0)
        state = first + fade1[h : h + 1] * (second + fade2[h : h + 1] * third)
        later = fade0[h : h + 1] * state + partner[rows, :].astype(f32)
        entering[rows, :] = jnp.where(zh == 0, state, later).astype(bf16)
    contract = (((1,), (1,)), ((), ()))
    wide = x[...].astype(f32)
    carried = widen(jnp.exp(down), SSM_HEAD_DIM) * lax.dot_general(
        out_rows[...], entering[...], contract, preferred_element_type=f32
    )
    rest = carried + widen(gain[...], SSM_HEAD_DIM) * wide
    affinity = lax.dot_general(
        out_rows[...], in_rows[...], contract, preferred_element_type=f32
    )
    row = lax.broadcasted_iota(jnp.int32, (length, length), 0)
    col = lax.broadcasted_iota(jnp.int32, (length, length), 1)
    causal = col <= row
    for h in range(heads):
        lanes = slice(h * SSM_HEAD_DIM, (h + 1) * SSM_HEAD_DIM)
        gaps = down[:, h : h + 1] - across[h : h + 1, :]
        mixing = affinity * jnp.exp(jnp.where(causal, gaps, masked_score))
        inside = jnp.dot(mixing.astype(bf16), x[:, lanes], preferred_element_type=f32)
        out[:, lanes] = (inside + rest[:, lanes]).astype(bf16)


def sum_body(count):
    def body(s, *refs):
        total = refs[0][...].astype(f32)
        for ref in refs[1:count]:
            total = total + ref[...].astype(f32)
        refs[count][...] = total.astype(bf16)

    return body


def on_device(
    scan_input,
    input_map,
    output_map,
    log_decay,
    skip_gain,
    query_rows,
    key_rows,
    value_rows,
    out_weight,
):
    tp = lax.axis_index("tp")
    core = tp % 2
    group = tp // (TP // GROUPS)
    shape = jax.ShapeDtypeStruct
    length = query_rows.shape[0]
    head_block = (length, HEAD_DIM)

    def columns(array, index):
        return lax.dynamic_slice_in_dim(array, index * HEAD_DIM, HEAD_DIM, 1)

    first = core == 0
    sent = jnp.where(first, columns(key_rows, group ^ 1), columns(value_rows, group ^ 1))
    arrived_pair = swap_zh_near(sent)
    own_keys, own_values = columns(key_rows, group), columns(value_rows, group)
    own = jnp.where(first, own_keys, own_values)
    in_rows, out_rows = columns(input_map, group), columns(output_map, group)

    (pair,) = call(
        join_body,
        [whole(head_block)] * 2,
        [shape((2 * length, HEAD_DIM), bf16)],
        (own, arrived_pair),
    )
    fetched = [shift_y(pair, d) for d in (2, 1, 3)]

    weight_block = (ROWS, out_weight.shape[1])
    sent_mate, own_weight = call(
        copy_body,
        [pl.BlockSpec(memory_space=pl.ANY)],
        [shape((CHIPS, *weight_block), bf16)] * 2,
        [out_weight.reshape(CHIPS, 2, *weight_block)],
        scratch=[pltpu.SemaphoreType.DMA((2,))],
        out_specs=[pl.BlockSpec(memory_space=pl.ANY)] * 2,
        after=[sent],
    )
    mate = swap_core(sent_mate)
    heads = log_decay.shape[1]
    inner = heads * SSM_HEAD_DIM
    state_shape = shape((inner + 2 * heads, N_STATE), bf16)
    x_spec = whole(scan_input.shape)
    decay_spec = whole(log_decay.shape)
    (closing,) = call(
        closing_body,
        [x_spec, whole(head_block), decay_spec],
        [state_shape],
        (scan_input, in_rows, log_decay),
        us=0.3,
    )

    stat = shape((2 * length, HEAD_DIM), f32)
    q_spec = whole(query_rows.shape)
    near_part = call(
        attend_near_body,
        [q_spec] + [whole(head_block)] * 2,
        [stat] * 3,
        (query_rows, own_keys, own_values),
        scratch=[pltpu.VMEM((2 * length, length), f32)],
        us=0.3,
    )
    (others,) = call(
        join_body,
        [whole(head_block)] + [whole(pair.shape)] * 3,
        [shape((7 * length, HEAD_DIM), bf16)],
        (arrived_pair, fetched[1], fetched[0], fetched[2]),
        after=[closing, near_part[0]],
    )
    others_there = swap_core(others)
    (attended,) = call(
        attend_far_body,
        [q_spec] + [whole(others.shape)] * 2 + [whole(stat.shape)] * 3,
        [shape((query_rows.shape[1], length), bf16)],
        (query_rows, others, others_there, *near_part),
        scratch=[pltpu.VMEM((2 * length, 7 * length), f32)],
        us=40,
    )
    attended_there = swap_core(attended)

    partner = swap_zh(closing)
    def project(offsets, after=()):
        return call(
            project_body(offsets),
            [whole(mate.shape)] * 2 + [whole(attended.shape)] * 2,
            [shape((2, 2, ROWS, length), bf16)] * 2,
            [own_weight, mate, attended, attended_there],
            after=after,
            us=1.3,
        )

    sent1, sent2 = project([4, 5, 8, 9, 14, 15, 10, 11])
    kept1, kept2 = project([0, 1, 12, 13, 2, 3, 6, 7], [sent1, out_rows])
    arrived1, arrived2 = swap_x(sent1, 1), swap_x(sent2, 3)

    def add_split(blocks, out):
        return call(
            add_split_body, [whole(block.shape) for block in blocks], [out] * 4, blocks
        )

    pair_rows = shape((2, ROWS, length), bf16)
    kept1, sent1, kept2, sent2 = add_split((kept1, arrived1, kept2, arrived2), pair_rows)
    arrived1, arrived2 = swap_x(sent1, 3), swap_x(sent2, 1)
    (joined,) = call(
        pair_body(heads),
        [whole(closing.shape)] * 2,
        [state_shape],
        (closing, partner),
        after=[sent1, sent2],
    )
    earlier = [shift_y(joined, d) for d in (2, 1, 3)]
    z0, z1, z2, z3 = add_split((kept1, arrived1, kept2, arrived2), shape((ROWS, length), bf16))
    arrived = [z0] + [swap_zl(z, b) for b, z in ((2, z2), (3, z3), (1, z1))]
    (attn_out,) = call(
        sum_body(4),
        [whole((ROWS, length))] * 4,
        [shape((ROWS, length), bf16)],
        arrived,
        us=1.3,
    )

    (ssm_out,) = call(
        scan_body,
        [x_spec, whole(head_block), whole(head_block), decay_spec, whole((1, heads))]
        + [whole(closing.shape)] * 4,
        [shape(scan_input.shape, bf16)],
        (
            scan_input,
            in_rows,
            out_rows,
            log_decay,
            skip_gain.reshape(1, heads),
            partner,
            earlier[1],
            earlier[0],
            earlier[2],
        ),
        scratch=[pltpu.VMEM((inner, N_STATE), bf16)],
        after=[z1, z3],
        us=3,
    )
    return (ssm_out, attn_out)


def solution(mesh):
    placed = (
        P("section", "tp"),
        P("section", None),
        P("section", None),
        P("section", "tp"),
        P("tp"),
        P("section", "tp"),
        P("section", None),
        P("section", None),
        P(None, "tp"),
    )
    return jax.shard_map(
        on_device,
        mesh=mesh,
        in_specs=placed,
        out_specs=(P("section", "tp"), P("tp", "section")),
        check_vma=False,
    )
```

```python
import math

import jax
import jax.numpy as jnp
from jax import lax
from jax.experimental import pallas as pl
from jax.experimental.pallas import tpu as pltpu
from jax.sharding import PartitionSpec as P

SCAN_HEADS = 256
SSM_HEAD_DIM = 64
N_STATE = 128
GROUPS = 8
Q_HEADS = 64
KV_HEADS = 8
HEAD_DIM = 128

SECTIONS = 8
TP = 32
ROWS = 256
CHIPS = 16
masked_score = -1e30
bf16 = jnp.bfloat16
f32 = jnp.float32


def swap_core(block):
    return lax.ppermute(block, "tp", [(t, t ^ 1) for t in range(TP)])


def swap_zh(block):
    return lax.ppermute(block, "section", [(s, s ^ 1) for s in range(SECTIONS)])


def shift_y(block, distance):
    route = [(s, (s + 2 * distance) % SECTIONS) for s in range(SECTIONS)]
    return lax.ppermute(block, "section", route)


def swap_zh_near(block):
    route = [
        (s * TP + t, (s ^ 1) * TP + (t ^ 4)) for s in range(SECTIONS) for t in range(TP)
    ]
    return lax.ppermute(block, ("section", "tp"), route)


def swap_x(block, offset):
    return lax.ppermute(block, "tp", [(t, t ^ (8 * offset)) for t in range(TP)])


def swap_zl(block, offset):
    return lax.ppermute(block, "tp", [(t, t ^ (2 * offset)) for t in range(TP)])


def whole(shape):
    return pl.BlockSpec(memory_space=pltpu.VMEM)


class Place:
    def __getitem__(self, item):
        if item < 2:
            section = lax.axis_index("section")
            return section >> 1 if item == 0 else section & 1
        tp = lax.axis_index("tp")
        return tp & 1 if item == 2 else (tp >> 1) ^ (item - 5)


def call(
    body, in_specs, out_shapes, args, scratch=(), limit=16, after=(), us=0.5, out_specs=None
):
    first, count = len(in_specs), len(after)

    def ordered(*refs):
        body(Place(), *refs[:first], *refs[first + count :])

    return pl.pallas_call(
        ordered,
        in_specs=list(in_specs) + [pl.BlockSpec(memory_space=pl.ANY)] * count,
        out_specs=out_specs or [whole(o.shape) for o in out_shapes],
        scratch_shapes=list(scratch),
        out_shape=out_shapes,
        compiler_params=pltpu.CompilerParams(vmem_limit_bytes=limit * 1024 * 1024),
        cost_estimate=pl.CostEstimate(
            flops=int(us * 1e9), bytes_accessed=int(us * 3.5e6), transcendentals=0
        ),
    )(*args, *after)


def copy_body(s, weights, mate, own, sems):
    copies = [
        pltpu.make_async_copy(weights.at[:, 1 - s[2]], mate, sems.at[0]),
        pltpu.make_async_copy(weights.at[:, s[2]], own, sems.at[1]),
    ]
    for copy in copies:
        copy.start()
    for copy in copies:
        copy.wait()


def join_body(s, *refs):
    at = 0
    for ref in refs[:-1]:
        refs[-1][at : at + ref.shape[0], :] = ref[...]
        at += ref.shape[0]


def fold(op, block, into=None):
    for at in range(0, block.shape[1], 128):
        part = block[:, at : at + 128]
        into = part if into is None else op(into, part)
    return into


def attend(s, q, keys, values, owners, scores):
    length = q.shape[0]
    me = s[0] * 2 + s[1]
    rate = 1.0 / math.sqrt(HEAD_DIM) * math.log2(math.e)
    stacked = jnp.concatenate([q[:, :HEAD_DIM], q[:, HEAD_DIM:]], axis=0)
    top = None
    for b, owner in enumerate(owners):
        at = slice(b * length, (b + 1) * length)
        got = lax.dot_general(
            stacked, keys[at, :], (((1,), (1,)), ((), ())), preferred_element_type=f32
        )
        if owner is None:
            row = lax.broadcasted_iota(jnp.int32, got.shape, 0) & (length - 1)
            col = lax.broadcasted_iota(jnp.int32, got.shape, 1)
            got = jnp.where(col <= row, got, masked_score)
        elif not isinstance(owner, int):
            got = got + jnp.where(owner < me, 0.0, masked_score).astype(f32)
        scores[:, at] = got
        top = fold(jnp.maximum, got, top)
    top = jnp.max(top, axis=1, keepdims=True) * rate
    total = None
    mixed = jnp.zeros(stacked.shape, f32)
    for b in range(len(owners)):
        at = slice(b * length, (b + 1) * length)
        weights = jnp.exp2(scores[:, at] * rate - top)
        total = fold(jnp.add, weights, total)
        mixed = mixed + jnp.dot(
            weights.astype(bf16), values[at, :], preferred_element_type=f32
        )
    return top, total, mixed


def attend_near_body(s, q, keys, values, tops, totals, mixeds, scores):
    top, total, mixed = attend(s, q, keys, values, [None], scores)
    tops[...] = jnp.broadcast_to(top, tops.shape)
    totals[...] = total
    mixeds[...] = mixed


def attend_far_body(s, q, mine, other, tops, totals, mixeds, out, scores):
    y, zh = s[0], s[1]
    length = q.shape[0]

    def run(keys, values, count):
        owners = [y * 2 + 1 - zh] + [-1] * (count - 1)
        far_top, far_total, far_mixed = attend(s, q, keys, values, owners, scores)
        near_top = tops[...][:, :1]
        top = jnp.maximum(near_top, far_top)
        near, far = jnp.exp2(near_top - top), jnp.exp2(far_top - top)
        total = jnp.sum(totals[...] * near + far_total * far, axis=1, keepdims=True)
        done = (mixeds[...] * near + far_mixed * far) / total
        out[:HEAD_DIM, :] = done[:length].T.astype(bf16)
        out[HEAD_DIM:, :] = done[length:].T.astype(bf16)

    for rank in range(SECTIONS // 2):
        for core in range(2):

            @pl.when((y == rank) & (s[2] == core))
            def _(rank=rank, core=core):
                keys, values = (mine, other) if core == 0 else (other, mine)
                run(keys, values, 1 + 2 * rank)


def project_body(offsets):
    def body(s, own, mate, here, there, *outs):
        for i, r in enumerate(offsets):
            outs[i // 2][i % 2] = (
                jnp.dot(own[s[5 + r]], here[...], preferred_element_type=f32)
                + jnp.dot(mate[s[5 + r]], there[...], preferred_element_type=f32)
            ).astype(bf16)

    return body


def add_split_body(s, kept1, arrived1, kept2, arrived2, *outs):
    half = len(outs) // 2
    for kept, arrived, pieces in (
        (kept1, arrived1, outs[:half]),
        (kept2, arrived2, outs[half:]),
    ):
        if half == 1:
            pieces[0][...] = (kept[...].astype(f32) + arrived[...].astype(f32)).astype(bf16)
        else:
            for i, out in enumerate(pieces):
                out[...] = (kept[i].astype(f32) + arrived[i].astype(f32)).astype(bf16)


def running_sums(decay):
    length = decay.shape[0]
    row = lax.broadcasted_iota(jnp.int32, (length, length), 0)
    col = lax.broadcasted_iota(jnp.int32, (length, length), 1)
    lower = (col <= row).astype(f32)
    down = jnp.dot(lower, decay, precision=lax.Precision.HIGHEST, preferred_element_type=f32)
    across = lax.dot_general(
        decay,
        lower,
        (((0,), (1,)), ((), ())),
        precision=lax.Precision.HIGHEST,
        preferred_element_type=f32,
    )
    return down, across


def widen(per_head, width):
    heads = per_head.shape[1]
    row = lax.broadcasted_iota(jnp.int32, (heads, heads * width), 0)
    col = lax.broadcasted_iota(jnp.int32, (heads, heads * width), 1)
    spread = ((col // width) == row).astype(f32)
    return jnp.dot(per_head, spread, precision=lax.Precision.HIGHEST, preferred_element_type=f32)


def closing_body(s, x, in_rows, decay, out):
    heads = decay.shape[1]
    inner = heads * SSM_HEAD_DIM
    length = x.shape[0]
    down, across = running_sums(decay[...])
    tail = widen(jnp.exp(down[length - 1 :, :] - down), SSM_HEAD_DIM)
    scaled = (x[...].astype(f32) * tail).astype(bf16)
    out[:inner, :] = lax.dot_general(
        scaled, in_rows[...], (((0,), (0,)), ((), ())), preferred_element_type=f32
    ).astype(bf16)
    fade = jnp.exp(across[:, length - 1 :])
    fade = jnp.broadcast_to(fade, (heads, N_STATE))
    high = fade.astype(bf16)
    out[inner : inner + 2 * heads, :] = jnp.concatenate(
        [high.astype(f32), fade - high.astype(f32)], axis=0
    ).astype(bf16)


def fades(state, inner, heads):
    both = state[inner : inner + 2 * heads, :].astype(f32)
    return both[:heads] + both[heads:]


def head_rows(h):
    return slice(h * SSM_HEAD_DIM, (h + 1) * SSM_HEAD_DIM)


def pair_body(heads):
    inner = heads * SSM_HEAD_DIM

    def body(s, mine, partner, out):
        def run(first, second):
            fade0 = fades(first, inner, heads)
            fade1 = fades(second, inner, heads)
            for h in range(heads):
                rows = head_rows(h)
                out[rows, :] = (
                    fade1[h : h + 1] * first[rows, :].astype(f32) + second[rows, :].astype(f32)
                ).astype(bf16)
            fade = fade0 * fade1
            high = fade.astype(bf16)
            out[inner : inner + 2 * heads, :] = jnp.concatenate(
                [high.astype(f32), fade - high.astype(f32)], axis=0
            ).astype(bf16)

        @pl.when(s[1] == 0)
        def _():
            run(mine, partner)

        @pl.when(s[1] != 0)
        def _():
            run(partner, mine)

    return body


def scan_body(s, x, in_rows, out_rows, decay, gain, partner, t1, t2, t3, out, entering):
    y, zh = s[0], s[1]
    heads = decay.shape[1]
    inner = heads * SSM_HEAD_DIM
    length = x.shape[0]
    down, across = running_sums(decay[...])
    fade1 = fades(t1, inner, heads)
    fade2 = fades(t2, inner, heads)
    fade0 = fades(partner, inner, heads)
    for h in range(heads):
        rows = head_rows(h)
        third = jnp.where(y >= 3, t3[rows, :].astype(f32), 0.0)
        second = jnp.where(y >= 2, t2[rows, :].astype(f32), 0.0)
        first = jnp.where(y >= 1, t1[rows, :].astype(f32), 0.0)
        state = first + fade1[h : h + 1] * (second + fade2[h : h + 1] * third)
        later = fade0[h : h + 1] * state + partner[rows, :].astype(f32)
        entering[rows, :] = jnp.where(zh == 0, state, later).astype(bf16)
    contract = (((1,), (1,)), ((), ()))
    wide = x[...].astype(f32)
    carried = widen(jnp.exp(down), SSM_HEAD_DIM) * lax.dot_general(
        out_rows[...], entering[...], contract, preferred_element_type=f32
    )
    rest = carried + widen(gain[...], SSM_HEAD_DIM) * wide
    affinity = lax.dot_general(
        out_rows[...], in_rows[...], contract, preferred_element_type=f32
    )
    row = lax.broadcasted_iota(jnp.int32, (length, length), 0)
    col = lax.broadcasted_iota(jnp.int32, (length, length), 1)
    causal = col <= row
    for h in range(heads):
        lanes = slice(h * SSM_HEAD_DIM, (h + 1) * SSM_HEAD_DIM)
        gaps = down[:, h : h + 1] - across[h : h + 1, :]
        mixing = affinity * jnp.exp(jnp.where(causal, gaps, masked_score))
        inside = jnp.dot(mixing.astype(bf16), x[:, lanes], preferred_element_type=f32)
        out[:, lanes] = (inside + rest[:, lanes]).astype(bf16)


def sum_body(count):
    def body(s, *refs):
        total = refs[0][...].astype(f32)
        for ref in refs[1:count]:
            total = total + ref[...].astype(f32)
        refs[count][...] = total.astype(bf16)

    return body


def on_device(
    scan_input,
    input_map,
    output_map,
    log_decay,
    skip_gain,
    query_rows,
    key_rows,
    value_rows,
    out_weight,
):
    tp = lax.axis_index("tp")
    core = tp % 2
    group = tp // (TP // GROUPS)
    shape = jax.ShapeDtypeStruct
    length = query_rows.shape[0]
    head_block = (length, HEAD_DIM)

    def columns(array, index):
        return lax.dynamic_slice_in_dim(array, index * HEAD_DIM, HEAD_DIM, 1)

    first = core == 0
    sent = jnp.where(first, columns(key_rows, group ^ 1), columns(value_rows, group ^ 1))
    arrived_pair = swap_zh_near(sent)
    own_keys, own_values = columns(key_rows, group), columns(value_rows, group)
    own = jnp.where(first, own_keys, own_values)
    in_rows, out_rows = columns(input_map, group), columns(output_map, group)

    (pair,) = call(
        join_body,
        [whole(head_block)] * 2,
        [shape((2 * length, HEAD_DIM), bf16)],
        (own, arrived_pair),
    )
    fetched = [shift_y(pair, d) for d in (2, 1, 3)]

    weight_block = (ROWS, out_weight.shape[1])
    sent_mate, own_weight = call(
        copy_body,
        [pl.BlockSpec(memory_space=pl.ANY)],
        [shape((CHIPS, *weight_block), bf16)] * 2,
        [out_weight.reshape(CHIPS, 2, *weight_block)],
        scratch=[pltpu.SemaphoreType.DMA((2,))],
        out_specs=[pl.BlockSpec(memory_space=pl.ANY)] * 2,
        after=[sent],
    )
    mate = swap_core(sent_mate)
    heads = log_decay.shape[1]
    inner = heads * SSM_HEAD_DIM
    state_shape = shape((inner + 2 * heads, N_STATE), bf16)
    x_spec = whole(scan_input.shape)
    decay_spec = whole(log_decay.shape)
    (closing,) = call(
        closing_body,
        [x_spec, whole(head_block), decay_spec],
        [state_shape],
        (scan_input, in_rows, log_decay),
        us=0.3,
    )

    stat = shape((2 * length, HEAD_DIM), f32)
    q_spec = whole(query_rows.shape)
    near_part = call(
        attend_near_body,
        [q_spec] + [whole(head_block)] * 2,
        [stat] * 3,
        (query_rows, own_keys, own_values),
        scratch=[pltpu.VMEM((2 * length, length), f32)],
        us=0.3,
    )
    (others,) = call(
        join_body,
        [whole(head_block)] + [whole(pair.shape)] * 3,
        [shape((7 * length, HEAD_DIM), bf16)],
        (arrived_pair, fetched[1], fetched[0], fetched[2]),
        after=[closing, near_part[0]],
    )
    others_there = swap_core(others)
    (attended,) = call(
        attend_far_body,
        [q_spec] + [whole(others.shape)] * 2 + [whole(stat.shape)] * 3,
        [shape((query_rows.shape[1], length), bf16)],
        (query_rows, others, others_there, *near_part),
        scratch=[pltpu.VMEM((2 * length, 7 * length), f32)],
        us=40,
    )
    attended_there = swap_core(attended)

    partner = swap_zh(closing)
    def project(offsets, after=()):
        return call(
            project_body(offsets),
            [whole(mate.shape)] * 2 + [whole(attended.shape)] * 2,
            [shape((2, ROWS, length), bf16)] * (len(offsets) // 2),
            [own_weight, mate, attended, attended_there],
            after=after,
            us=1.3,
        )

    sent1, sent3 = project([5, 9, 15, 11])
    sent0, sent2 = project([4, 8, 14, 10], [sent1])
    kept1, kept3, kept0, kept2 = project([1, 13, 3, 7, 0, 12, 2, 6], [sent0, out_rows])

    def add_split(blocks, pieces):
        out = shape((ROWS, length), bf16)
        return call(
            add_split_body, [whole(block.shape) for block in blocks], [out] * pieces, blocks
        )

    def halve(kept, sent, kept_too, sent_too):
        kept, sent, kept_too, sent_too = add_split(
            (kept, swap_x(sent, 1), kept_too, swap_x(sent_too, 3)), 4
        )
        return kept, sent, kept_too, sent_too

    kept1, sent1, kept3, sent3 = halve(kept1, sent1, kept3, sent3)
    kept0, sent0, kept2, sent2 = halve(kept0, sent0, kept2, sent2)
    z1, z3 = add_split((kept1, swap_x(sent1, 3), kept3, swap_x(sent3, 1)), 2)
    z0, z2 = add_split((kept0, swap_x(sent0, 3), kept2, swap_x(sent2, 1)), 2)
    (joined,) = call(
        pair_body(heads),
        [whole(closing.shape)] * 2,
        [state_shape],
        (closing, partner),
        after=[sent0, sent2],
    )
    earlier = [shift_y(joined, d) for d in (2, 1, 3)]
    arrived = [z0] + [swap_zl(z, b) for b, z in ((3, z3), (1, z1), (2, z2))]
    (attn_out,) = call(
        sum_body(4),
        [whole((ROWS, length))] * 4,
        [shape((ROWS, length), bf16)],
        arrived,
        us=1.3,
    )

    (ssm_out,) = call(
        scan_body,
        [x_spec, whole(head_block), whole(head_block), decay_spec, whole((1, heads))]
        + [whole(closing.shape)] * 4,
        [shape(scan_input.shape, bf16)],
        (
            scan_input,
            in_rows,
            out_rows,
            log_decay,
            skip_gain.reshape(1, heads),
            partner,
            earlier[1],
            earlier[0],
            earlier[2],
        ),
        scratch=[pltpu.VMEM((inner, N_STATE), bf16)],
        after=[z1, z3],
        us=3,
    )
    return (ssm_out, attn_out)


def solution(mesh):
    placed = (
        P("section", "tp"),
        P("section", None),
        P("section", None),
        P("section", "tp"),
        P("tp"),
        P("section", "tp"),
        P("section", None),
        P("section", None),
        P(None, "tp"),
    )
    return jax.shard_map(
        on_device,
        mesh=mesh,
        in_specs=placed,
        out_specs=(P("section", "tp"), P("tp", "section")),
        check_vma=False,
    )
```

```python
import math

import jax
import jax.numpy as jnp
from jax import lax
from jax.experimental import pallas as pl
from jax.experimental.pallas import tpu as pltpu
from jax.sharding import PartitionSpec as P

SCAN_HEADS = 256
SSM_HEAD_DIM = 64
N_STATE = 128
GROUPS = 8
Q_HEADS = 64
KV_HEADS = 8
HEAD_DIM = 128

SECTIONS = 8
TP = 32
ROWS = 256
CHIPS = 16
masked_score = -1e30
bf16 = jnp.bfloat16
f32 = jnp.float32


def swap_core(block):
    return lax.ppermute(block, "tp", [(t, t ^ 1) for t in range(TP)])


def swap_zh(block):
    return lax.ppermute(block, "section", [(s, s ^ 1) for s in range(SECTIONS)])


def shift_y(block, distance):
    route = [(s, (s + 2 * distance) % SECTIONS) for s in range(SECTIONS)]
    return lax.ppermute(block, "section", route)


def swap_zh_near(block):
    route = [
        (s * TP + t, (s ^ 1) * TP + (t ^ 4)) for s in range(SECTIONS) for t in range(TP)
    ]
    return lax.ppermute(block, ("section", "tp"), route)


def swap_x(block, offset):
    return lax.ppermute(block, "tp", [(t, t ^ (8 * offset)) for t in range(TP)])


def swap_zl(block, offset):
    return lax.ppermute(block, "tp", [(t, t ^ (2 * offset)) for t in range(TP)])


def whole(shape):
    return pl.BlockSpec(memory_space=pltpu.VMEM)


class Place:
    def __getitem__(self, item):
        if item < 2:
            section = lax.axis_index("section")
            return section >> 1 if item == 0 else section & 1
        tp = lax.axis_index("tp")
        return tp & 1 if item == 2 else (tp >> 1) ^ (item - 5)


def call(
    body, in_specs, out_shapes, args, scratch=(), limit=16, after=(), us=0.5, out_specs=None
):
    first, count = len(in_specs), len(after)

    def ordered(*refs):
        body(Place(), *refs[:first], *refs[first + count :])

    return pl.pallas_call(
        ordered,
        in_specs=list(in_specs) + [pl.BlockSpec(memory_space=pl.ANY)] * count,
        out_specs=out_specs or [whole(o.shape) for o in out_shapes],
        scratch_shapes=list(scratch),
        out_shape=out_shapes,
        compiler_params=pltpu.CompilerParams(vmem_limit_bytes=limit * 1024 * 1024),
        cost_estimate=pl.CostEstimate(
            flops=int(us * 1e9), bytes_accessed=int(us * 3.5e6), transcendentals=0
        ),
    )(*args, *after)


def copy_body(s, weights, mate, own, sems):
    copies = [
        pltpu.make_async_copy(weights.at[:, 1 - s[2]], mate, sems.at[0]),
        pltpu.make_async_copy(weights.at[:, s[2]], own, sems.at[1]),
    ]
    for copy in copies:
        copy.start()
    for copy in copies:
        copy.wait()


def join_body(s, *refs):
    at = 0
    for ref in refs[:-1]:
        refs[-1][at : at + ref.shape[0], :] = ref[...]
        at += ref.shape[0]


def fold(op, block, into=None):
    for at in range(0, block.shape[1], 128):
        part = block[:, at : at + 128]
        into = part if into is None else op(into, part)
    return into


def attend(s, q, keys, values, owners, scores):
    length = q.shape[0]
    me = s[0] * 2 + s[1]
    rate = 1.0 / math.sqrt(HEAD_DIM) * math.log2(math.e)
    stacked = jnp.concatenate([q[:, :HEAD_DIM], q[:, HEAD_DIM:]], axis=0)
    top = None
    for b, owner in enumerate(owners):
        at = slice(b * length, (b + 1) * length)
        got = lax.dot_general(
            stacked, keys[at, :], (((1,), (1,)), ((), ())), preferred_element_type=f32
        )
        if owner is None:
            row = lax.broadcasted_iota(jnp.int32, got.shape, 0) & (length - 1)
            col = lax.broadcasted_iota(jnp.int32, got.shape, 1)
            got = jnp.where(col <= row, got, masked_score)
        elif not isinstance(owner, int):
            got = got + jnp.where(owner < me, 0.0, masked_score).astype(f32)
        scores[:, at] = got
        top = fold(jnp.maximum, got, top)
    top = jnp.max(top, axis=1, keepdims=True) * rate
    total = None
    mixed = jnp.zeros(stacked.shape, f32)
    for b in range(len(owners)):
        at = slice(b * length, (b + 1) * length)
        weights = jnp.exp2(scores[:, at] * rate - top)
        total = fold(jnp.add, weights, total)
        mixed = mixed + jnp.dot(
            weights.astype(bf16), values[at, :], preferred_element_type=f32
        )
    return top, total, mixed


def attend_near_body(s, q, keys, values, tops, totals, mixeds, scores):
    top, total, mixed = attend(s, q, keys, values, [None], scores)
    tops[...] = jnp.broadcast_to(top, tops.shape)
    totals[...] = total
    mixeds[...] = mixed


def attend_far_body(s, q, mine, other, tops, totals, mixeds, out, scores):
    y, zh = s[0], s[1]
    length = q.shape[0]

    def run(keys, values, count):
        owners = [y * 2 + 1 - zh] + [-1] * (count - 1)
        far_top, far_total, far_mixed = attend(s, q, keys, values, owners, scores)
        near_top = tops[...][:, :1]
        top = jnp.maximum(near_top, far_top)
        near, far = jnp.exp2(near_top - top), jnp.exp2(far_top - top)
        total = jnp.sum(totals[...] * near + far_total * far, axis=1, keepdims=True)
        done = (mixeds[...] * near + far_mixed * far) / total
        out[:HEAD_DIM, :] = done[:length].T.astype(bf16)
        out[HEAD_DIM:, :] = done[length:].T.astype(bf16)

    for rank in range(SECTIONS // 2):
        for core in range(2):

            @pl.when((y == rank) & (s[2] == core))
            def _(rank=rank, core=core):
                keys, values = (mine, other) if core == 0 else (other, mine)
                run(keys, values, 1 + 2 * rank)


def project_body(offsets):
    def body(s, own, mate, here, there, *outs):
        each = len(offsets) // len(outs)
        for i, r in enumerate(offsets):
            outs[i // each][(i % each) // 2, i % 2] = (
                jnp.dot(own[s[5 + r]], here[...], preferred_element_type=f32)
                + jnp.dot(mate[s[5 + r]], there[...], preferred_element_type=f32)
            ).astype(bf16)

    return body


def add_split_body(s, kept1, arrived1, kept2, arrived2, *outs):
    half = len(outs) // 2
    for kept, arrived, pieces in (
        (kept1, arrived1, outs[:half]),
        (kept2, arrived2, outs[half:]),
    ):
        for i, out in enumerate(pieces):
            out[...] = (kept[i].astype(f32) + arrived[i].astype(f32)).astype(bf16)


def running_sums(decay):
    length = decay.shape[0]
    row = lax.broadcasted_iota(jnp.int32, (length, length), 0)
    col = lax.broadcasted_iota(jnp.int32, (length, length), 1)
    lower = (col <= row).astype(f32)
    down = jnp.dot(lower, decay, precision=lax.Precision.HIGHEST, preferred_element_type=f32)
    across = lax.dot_general(
        decay,
        lower,
        (((0,), (1,)), ((), ())),
        precision=lax.Precision.HIGHEST,
        preferred_element_type=f32,
    )
    return down, across


def widen(per_head, width):
    heads = per_head.shape[1]
    row = lax.broadcasted_iota(jnp.int32, (heads, heads * width), 0)
    col = lax.broadcasted_iota(jnp.int32, (heads, heads * width), 1)
    spread = ((col // width) == row).astype(f32)
    return jnp.dot(per_head, spread, precision=lax.Precision.HIGHEST, preferred_element_type=f32)


def closing_body(s, x, in_rows, decay, out):
    heads = decay.shape[1]
    inner = heads * SSM_HEAD_DIM
    length = x.shape[0]
    down, across = running_sums(decay[...])
    tail = widen(jnp.exp(down[length - 1 :, :] - down), SSM_HEAD_DIM)
    scaled = (x[...].astype(f32) * tail).astype(bf16)
    out[:inner, :] = lax.dot_general(
        scaled, in_rows[...], (((0,), (0,)), ((), ())), preferred_element_type=f32
    ).astype(bf16)
    fade = jnp.exp(across[:, length - 1 :])
    fade = jnp.broadcast_to(fade, (heads, N_STATE))
    high = fade.astype(bf16)
    out[inner : inner + 2 * heads, :] = jnp.concatenate(
        [high.astype(f32), fade - high.astype(f32)], axis=0
    ).astype(bf16)


def fades(state, inner, heads):
    both = state[inner : inner + 2 * heads, :].astype(f32)
    return both[:heads] + both[heads:]


def head_rows(h):
    return slice(h * SSM_HEAD_DIM, (h + 1) * SSM_HEAD_DIM)


def pair_body(heads):
    inner = heads * SSM_HEAD_DIM

    def body(s, mine, partner, out):
        def run(first, second):
            fade0 = fades(first, inner, heads)
            fade1 = fades(second, inner, heads)
            for h in range(heads):
                rows = head_rows(h)
                out[rows, :] = (
                    fade1[h : h + 1] * first[rows, :].astype(f32) + second[rows, :].astype(f32)
                ).astype(bf16)
            fade = fade0 * fade1
            high = fade.astype(bf16)
            out[inner : inner + 2 * heads, :] = jnp.concatenate(
                [high.astype(f32), fade - high.astype(f32)], axis=0
            ).astype(bf16)

        @pl.when(s[1] == 0)
        def _():
            run(mine, partner)

        @pl.when(s[1] != 0)
        def _():
            run(partner, mine)

    return body


def scan_body(s, x, in_rows, out_rows, decay, gain, partner, t1, t2, t3, out, entering):
    y, zh = s[0], s[1]
    heads = decay.shape[1]
    inner = heads * SSM_HEAD_DIM
    length = x.shape[0]
    down, across = running_sums(decay[...])
    fade1 = fades(t1, inner, heads)
    fade2 = fades(t2, inner, heads)
    fade0 = fades(partner, inner, heads)
    for h in range(heads):
        rows = head_rows(h)
        third = jnp.where(y >= 3, t3[rows, :].astype(f32), 0.0)
        second = jnp.where(y >= 2, t2[rows, :].astype(f32), 0.0)
        first = jnp.where(y >= 1, t1[rows, :].astype(f32), 0.0)
        state = first + fade1[h : h + 1] * (second + fade2[h : h + 1] * third)
        later = fade0[h : h + 1] * state + partner[rows, :].astype(f32)
        entering[rows, :] = jnp.where(zh == 0, state, later).astype(bf16)
    contract = (((1,), (1,)), ((), ()))
    wide = x[...].astype(f32)
    carried = widen(jnp.exp(down), SSM_HEAD_DIM) * lax.dot_general(
        out_rows[...], entering[...], contract, preferred_element_type=f32
    )
    rest = carried + widen(gain[...], SSM_HEAD_DIM) * wide
    affinity = lax.dot_general(
        out_rows[...], in_rows[...], contract, preferred_element_type=f32
    )
    row = lax.broadcasted_iota(jnp.int32, (length, length), 0)
    col = lax.broadcasted_iota(jnp.int32, (length, length), 1)
    causal = col <= row
    for h in range(heads):
        lanes = slice(h * SSM_HEAD_DIM, (h + 1) * SSM_HEAD_DIM)
        gaps = down[:, h : h + 1] - across[h : h + 1, :]
        mixing = affinity * jnp.exp(jnp.where(causal, gaps, masked_score))
        inside = jnp.dot(mixing.astype(bf16), x[:, lanes], preferred_element_type=f32)
        out[:, lanes] = (inside + rest[:, lanes]).astype(bf16)


def sum_body(count):
    def body(s, *refs):
        total = refs[0][...].astype(f32)
        for ref in refs[1:count]:
            total = total + ref[...].astype(f32)
        refs[count][...] = total.astype(bf16)

    return body


def on_device(
    scan_input,
    input_map,
    output_map,
    log_decay,
    skip_gain,
    query_rows,
    key_rows,
    value_rows,
    out_weight,
):
    tp = lax.axis_index("tp")
    core = tp % 2
    group = tp // (TP // GROUPS)
    shape = jax.ShapeDtypeStruct
    length = query_rows.shape[0]
    head_block = (length, HEAD_DIM)

    def columns(array, index):
        return lax.dynamic_slice_in_dim(array, index * HEAD_DIM, HEAD_DIM, 1)

    first = core == 0
    sent = jnp.where(first, columns(key_rows, group ^ 1), columns(value_rows, group ^ 1))
    arrived_pair = swap_zh_near(sent)
    own_keys, own_values = columns(key_rows, group), columns(value_rows, group)
    own = jnp.where(first, own_keys, own_values)
    in_rows, out_rows = columns(input_map, group), columns(output_map, group)

    (pair,) = call(
        join_body,
        [whole(head_block)] * 2,
        [shape((2 * length, HEAD_DIM), bf16)],
        (own, arrived_pair),
    )
    fetched = [shift_y(pair, d) for d in (2, 1, 3)]

    weight_block = (ROWS, out_weight.shape[1])
    sent_mate, own_weight = call(
        copy_body,
        [pl.BlockSpec(memory_space=pl.ANY)],
        [shape((CHIPS, *weight_block), bf16)] * 2,
        [out_weight.reshape(CHIPS, 2, *weight_block)],
        scratch=[pltpu.SemaphoreType.DMA((2,))],
        out_specs=[pl.BlockSpec(memory_space=pl.ANY)] * 2,
        after=[sent],
    )
    mate = swap_core(sent_mate)
    heads = log_decay.shape[1]
    inner = heads * SSM_HEAD_DIM
    state_shape = shape((inner + 2 * heads, N_STATE), bf16)
    x_spec = whole(scan_input.shape)
    decay_spec = whole(log_decay.shape)
    (closing,) = call(
        closing_body,
        [x_spec, whole(head_block), decay_spec],
        [state_shape],
        (scan_input, in_rows, log_decay),
        us=0.3,
    )

    stat = shape((2 * length, HEAD_DIM), f32)
    q_spec = whole(query_rows.shape)
    near_part = call(
        attend_near_body,
        [q_spec] + [whole(head_block)] * 2,
        [stat] * 3,
        (query_rows, own_keys, own_values),
        scratch=[pltpu.VMEM((2 * length, length), f32)],
        us=0.3,
    )
    (others,) = call(
        join_body,
        [whole(head_block)] + [whole(pair.shape)] * 3,
        [shape((7 * length, HEAD_DIM), bf16)],
        (arrived_pair, fetched[1], fetched[0], fetched[2]),
        after=[closing, near_part[0], own_weight],
    )
    others_there = swap_core(others)
    (attended,) = call(
        attend_far_body,
        [q_spec] + [whole(others.shape)] * 2 + [whole(stat.shape)] * 3,
        [shape((query_rows.shape[1], length), bf16)],
        (query_rows, others, others_there, *near_part),
        scratch=[pltpu.VMEM((2 * length, 7 * length), f32)],
        us=40,
    )
    attended_there = swap_core(attended)

    partner = swap_zh(closing)
    def project(offsets, after=()):
        return call(
            project_body(offsets),
            [whole(mate.shape)] * 2 + [whole(attended.shape)] * 2,
            [shape((2, 2, ROWS, length), bf16)] * 2,
            [own_weight, mate, attended, attended_there],
            after=after,
            us=1.3,
        )

    sent1, sent2 = project([4, 5, 8, 9, 14, 15, 10, 11])
    kept1, kept2 = project([0, 1, 12, 13, 2, 3, 6, 7], [sent1, out_rows])
    arrived1, arrived2 = swap_x(sent1, 1), swap_x(sent2, 3)

    def add_split(blocks, out):
        return call(
            add_split_body, [whole(block.shape) for block in blocks], [out] * 4, blocks
        )

    pair_rows = shape((2, ROWS, length), bf16)
    kept1, sent1, kept2, sent2 = add_split((kept1, arrived1, kept2, arrived2), pair_rows)
    arrived1, arrived2 = swap_x(sent1, 3), swap_x(sent2, 1)
    (joined,) = call(
        pair_body(heads),
        [whole(closing.shape)] * 2,
        [state_shape],
        (closing, partner),
        after=[sent1, sent2],
    )
    earlier = [shift_y(joined, d) for d in (2, 1, 3)]
    z0, z1, z2, z3 = add_split((kept1, arrived1, kept2, arrived2), shape((ROWS, length), bf16))
    arrived = [z0] + [swap_zl(z, b) for b, z in ((2, z2), (3, z3), (1, z1))]
    (attn_out,) = call(
        sum_body(4),
        [whole((ROWS, length))] * 4,
        [shape((ROWS, length), bf16)],
        arrived,
        us=1.3,
    )

    (ssm_out,) = call(
        scan_body,
        [x_spec, whole(head_block), whole(head_block), decay_spec, whole((1, heads))]
        + [whole(closing.shape)] * 4,
        [shape(scan_input.shape, bf16)],
        (
            scan_input,
            in_rows,
            out_rows,
            log_decay,
            skip_gain.reshape(1, heads),
            partner,
            earlier[1],
            earlier[0],
            earlier[2],
        ),
        scratch=[pltpu.VMEM((inner, N_STATE), bf16)],
        after=[z1, z3],
        us=3,
    )
    return (ssm_out, attn_out)


def solution(mesh):
    placed = (
        P("section", "tp"),
        P("section", None),
        P("section", None),
        P("section", "tp"),
        P("tp"),
        P("section", "tp"),
        P("section", None),
        P("section", None),
        P(None, "tp"),
    )
    return jax.shard_map(
        on_device,
        mesh=mesh,
        in_specs=placed,
        out_specs=(P("section", "tp"), P("tp", "section")),
        check_vma=False,
    )
```
